256 devices in a mesh: row: 16 (over y, z_hi, core), col: 16 (over x, z_lo).
Axes of the slice: x: 4, y: 4, z: 8 (z_hi: 2, z_lo: 4; z = z_hi * 4 + z_lo), core: 2. Of those that a mesh axis runs over, the one named last changes fastest.
Arguments:
- pair: bfloat16 [1024, 1024, 128], P('row', 'col'), may hold values from -6 to 6
- norm_gain: float32 [128], replicated, may hold values from 0.1 to 1.9
- norm_shift: float32 [128], replicated, may hold values from -3 to 3
- w_query: bfloat16 [128, 128], replicated, may hold values from -1 to 1
- w_key: bfloat16 [128, 128], replicated, may hold values from -0.5 to 0.5
- w_value: bfloat16 [128, 128], replicated, may hold values from -0.5 to 0.5
- w_gate: bfloat16 [128, 128], replicated, may hold values from -0.5 to 0.5
- gate_shift: float32 [128], replicated, may hold values from -1 to 1
- w_bias: float32 [128, 4], replicated, may hold values from -30 to 30
- w_out: bfloat16 [128, 128], replicated, may hold values from -1 to 1
- out_shift: float32 [128], replicated, may hold values from -3 to 3
Outputs:
- update: bfloat16 [1024, 1024, 128], P('row', 'col')
The draws below stay inside these ranges and needn't reach their ends.
All inputs are finite; a program needn't handle non-finite values.
Results may differ from the reference program's by a relative error of at most 0.0015.
The reference program's roundings to bfloat16 on the way (of `normed`, `query`, `weights` and `gated`) count: a program that leaves them out, or rounds other values in their place, can miss the bound.
Values may be sent and summed in bfloat16 or wider, within the bound.
No kernel may reach another device: no remote copies, remote signals or barrier semaphores. Data moves between devices by JAX's collectives and lax.ppermute only.
A program may use at most 128 MiB of HBM per device.

```python
import math
import jax
import jax.numpy as jnp
from jax import lax

N = 1024
C = 128
H = 4
DH = 32


def draw_w_bias(key, part):
    first, second = jax.random.split(jax.random.fold_in(key, 17))
    base = jax.random.truncated_normal(first, -3.0, 3.0, (C, H), jnp.float32) / math.sqrt(C)
    scales = jnp.exp(jax.random.uniform(second, (H,), jnp.float32, math.log(0.5), math.log(2.0)))
    return base * scales[None, :]


def level_of(stream_key, dims, pieces, least, top_value):
    factor_of = 1.0
    for axis_at, shards_of in pieces:
        heights = jax.random.uniform(jax.random.fold_in(jax.random.fold_in(stream_key, 6), axis_at), (shards_of,), jnp.float32, least / len(pieces), top_value / len(pieces))
        factor_of = factor_of * jnp.repeat(jnp.exp(heights), dims[axis_at] // shards_of).reshape((-1,) + (1,) * (len(dims) - 1 - axis_at))
    return factor_of


def gaussian(key, shape, scale, most, pieces=(), dtype=jnp.bfloat16):
    entries = scale * jax.random.normal(key, shape, jnp.float32)
    if pieces:
        entries = entries * level_of(key, shape, pieces, -0.22, 0.18)
    return jnp.clip(entries, -most, most).astype(dtype)


def setup_inputs(seed: int = 0) -> dict:
    key_of = jax.random.split(jax.random.key(seed), 12)
    return {
        "pair": gaussian(key_of[0], (N, N, C), 1.0, 6.0, ((0, 16), (1, 16))),
        "norm_gain": jnp.clip(1.0 + 0.18 * jax.random.normal(key_of[1], (C,), jnp.float32), 0.1, 1.9),
        "norm_shift": gaussian(key_of[2], (C,), 0.3, 3.0, (), jnp.float32),
        "w_query": gaussian(key_of[3], (C, H * DH), 0.18, 1.0),
        "w_key": gaussian(key_of[4], (C, H * DH), C ** -0.5, 0.5),
        "w_value": gaussian(key_of[5], (C, H * DH), C ** -0.5, 0.5),
        "w_gate": gaussian(key_of[6], (C, H * DH), C ** -0.5, 0.5),
        "gate_shift": jnp.clip(jax.random.uniform(key_of[7], (H * DH,), jnp.float32, -1.0, 1.0), -1.0, 1.0),
        "w_bias": draw_w_bias(jax.random.fold_in(key_of[11], 71), 0),
        "w_out": gaussian(key_of[9], (H * DH, C), (H * DH // 4) ** -0.5, 1.0),
        "out_shift": gaussian(key_of[10], (C,), 0.5, 3.0, (), jnp.float32),
    }


def normalize(values, gain, shift):
    values = values.astype(jnp.float32)
    mean = lax.optimization_barrier(jnp.mean(values, axis=-1, keepdims=True))
    centred = values - mean
    spread = lax.optimization_barrier(jnp.mean(centred * centred, axis=-1, keepdims=True))
    return (centred * lax.rsqrt(spread + 1e-05) * gain + shift).astype(jnp.bfloat16)

def reference(pair, norm_gain, norm_shift, w_query, w_key, w_value, w_gate, gate_shift, w_bias, w_out, out_shift):
    normed = normalize(pair, norm_gain, norm_shift)
    bias = jnp.einsum('jkc,ch->hjk', normed.astype(jnp.float32), w_bias, precision=lax.Precision.HIGHEST)
    heads = w_bias.shape[1]
    inner = w_query.shape[1]
    depth = inner // heads
    seq_length = normed.shape[1]

    def one_row(pair_row):
        query = (jnp.dot(pair_row, w_query, preferred_element_type=jnp.float32) * (1.0 / math.sqrt(depth))).astype(jnp.bfloat16)
        key = jnp.dot(pair_row, w_key, preferred_element_type=jnp.float32).astype(jnp.bfloat16)
        value = jnp.dot(pair_row, w_value, preferred_element_type=jnp.float32).astype(jnp.bfloat16)
        gate = jax.nn.sigmoid(jnp.dot(pair_row, w_gate, preferred_element_type=jnp.float32) + gate_shift)
        query = query.reshape(seq_length, heads, depth).astype(jnp.float32)
        key = key.reshape(seq_length, heads, depth).astype(jnp.float32)
        value = value.reshape(seq_length, heads, depth).astype(jnp.float32)
        scores = jnp.einsum('jhd,khd->hjk', query, key) + bias
        largest = lax.optimization_barrier(jnp.max(scores, axis=2, keepdims=True))
        raised = jnp.exp(scores - largest)
        weights = (raised / lax.optimization_barrier(jnp.sum(raised, axis=2, keepdims=True))).astype(jnp.bfloat16)
        attended = jnp.einsum('hjk,khd->jhd', weights.astype(jnp.float32), value).reshape(seq_length, inner)
        gated = (gate * attended).astype(jnp.bfloat16)
        return (jnp.dot(gated, w_out, preferred_element_type=jnp.float32) + out_shift).astype(jnp.bfloat16)
    return lax.map(one_row, normed)
```

```python
import functools, math
import jax, jax.numpy as jnp
from jax import lax
from jax.sharding import PartitionSpec as P
from jax.experimental import pallas as pl
from jax.experimental.pallas import tpu as pltpu

F32 = jnp.float32
BF = jnp.bfloat16
CHUNKS = 2
def dot_t(a,b):
    return lax.dot_general(a,b,(((1,),(1,)),((),())),preferred_element_type=F32)

def attend_kernel(depth, at, x0,x1,x2,x3, b00,b01,b10,b11,b20,b21,b30,b31, wk,wvT,wqT,wgT,gsh,wo,osh, out, k_ref, v_ref, s_ref):
    xs=(x0,x1,x2,x3)
    bias=((b00,b01),(b10,b11),(b20,b21),(b30,b31))
    y=at[0]; z=at[1]; zl=at[2]; core=at[3]
    pieces=[]
    for b in range(2):
        half=lax.rem(core+b,2)
        for s in range(4):
            for t in range(4):
                pieces.append(xs[t][s,0,pl.ds(pl.multiple_of(half*32,32),32),:])
    xk=jnp.concatenate(pieces,axis=0)
    k_ref[...]=jnp.dot(xk,wk[...],preferred_element_type=F32).astype(BF)
    v_ref[...]=dot_t(wvT[...],xk).astype(BF)
    slot=[lax.rem(zl+4-qb,4) for qb in range(4)]
    xq=jnp.concatenate([x0[slot[qb],0] for qb in range(4)],axis=0)
    qT=(dot_t(wqT[...],xq)*(1.0/math.sqrt(depth))).astype(BF)
    gate=jax.nn.sigmoid(dot_t(wgT[...],xq)+gsh[...])
    rows=lax.broadcasted_iota(jnp.int32,qT.shape,0)//depth
    zslot=[[lax.rem(z+8-(zh*4+lax.rem(zl+4-s,4)),8) for s in range(4)] for zh in range(2)]
    parts=[]
    for a in range(4):
        h=lax.rem(y+4-a,4)
        qm=jnp.where(rows==h,qT,jnp.zeros_like(qT))
        top=None
        for b in range(2):
            for s in range(4):
                c=b*4+s
                sc=jnp.dot(k_ref[c*128:(c+1)*128,:],qm,preferred_element_type=F32)
                sc=sc+jnp.concatenate([bias[a][b][zslot[zh][s]] for zh in range(2)],axis=1)
                s_ref[a%2,c]=sc
                m=jnp.max(sc.reshape(16,8,256),axis=0)
                top=m if top is None else jnp.maximum(top,m)
        top=jnp.max(top,axis=0,keepdims=True)
        tot=None
        for c in range(8):
            e=jnp.exp(s_ref[a%2,c]-top)
            s_ref[a%2,c]=e
            m=jnp.sum(e.reshape(16,8,256),axis=0)
            tot=m if tot is None else tot+m
        inv=1.0/jnp.sum(tot,axis=0,keepdims=True)
        acc=None
        vh=v_ref[pl.ds(pl.multiple_of(h*depth,depth),depth),:]
        w=[(s_ref[a%2,c]*inv).astype(BF) for c in range(8)]
        acc=jnp.dot(vh,jnp.concatenate(w,axis=0),preferred_element_type=F32)
        parts.append((h,acc))
    for h,acc in parts:
        s_ref[0,0,pl.ds(pl.multiple_of(h*depth,depth),depth),:]=acc
    gated=(gate*s_ref[0,0]).astype(BF)
    upd=lax.dot_general(gated,wo[...],(((0,),(0,)),((),())),preferred_element_type=F32)+osh[...]
    upd=upd.astype(BF)
    for qb in range(4):
        out[slot[qb],0]=upd[qb*64:(qb+1)*64]

def attend(at, xs, biases, wk,wvT,wqT,wgT,gsh,wo,osh, kernel=attend_kernel, extra=()):
    R=xs[0].shape[1]
    xspec=pl.BlockSpec((4,1,64,128),lambda i,at:(0,i,0,0))
    bspec=pl.BlockSpec((8,128,128),lambda i,at:(0,0,0))
    full=lambda a: pl.BlockSpec(a.shape,lambda i,at:(0,)*a.ndim)
    ws=(wk,wvT,wqT,wgT,gsh,wo,osh)
    return pl.pallas_call(functools.partial(kernel,32),
        out_shape=jax.ShapeDtypeStruct((4,R,64,128),BF),
        grid_spec=pltpu.PrefetchScalarGridSpec(num_scalar_prefetch=1,grid=(R,),
            in_specs=[xspec]*4+[bspec]*8+[full(w) for w in ws],
            out_specs=xspec,
            scratch_shapes=[pltpu.VMEM((1024,128),BF),pltpu.VMEM((128,1024),BF),pltpu.VMEM((2,8,128,256),F32),*extra]),
        compiler_params=pltpu.CompilerParams(vmem_limit_bytes=48<<20,dimension_semantics=("arbitrary",)),
        cost_estimate=pl.CostEstimate(flops=R*300_000_000,bytes_accessed=R*(1<<20),transcendentals=R*(1<<20)),
    )(at,*xs,*[b for p in biases for b in p],*ws)


def normalize(values, gain, shift):
    values = values.astype(F32)
    mean = jnp.mean(values, axis=-1, keepdims=True)
    centred = values - mean
    spread = jnp.mean(centred * centred, axis=-1, keepdims=True)
    return (centred * lax.rsqrt(spread + 1e-05) * gain + shift).astype(BF)


AXES = ("row", "col")


def move(array, to):
    pairs = []
    for source in range(256):
        row, col = divmod(source, 16)
        y, zh, core = row // 4, row // 2 % 2, row % 2
        x, zl = divmod(col, 4)
        y, z, core, x = to(y, zh * 4 + zl, core, x)
        y, z, x = y % 4, z % 8, x % 4
        target = ((y * 2 + z // 4) * 2 + core) * 16 + x * 4 + z % 4
        pairs.append((source, target))
    return lax.ppermute(array, AXES, pairs)


def turn(z, step):
    return z // 4 * 4 + (z + step) % 4


def on_device(
    pair,
    norm_gain,
    norm_shift,
    w_query,
    w_key,
    w_value,
    w_gate,
    gate_shift,
    w_bias,
    w_out,
    out_shift,
):
    row, col = lax.axis_index("row"), lax.axis_index("col")
    y, zh, core = row // 4, row // 2 % 2, row % 2
    x, zl = col // 4, col % 4
    z = zh * 4 + zl
    place = jnp.stack([y, z, zl, core]).astype(jnp.int32)
    normed = normalize(pair, norm_gain, norm_shift)
    with jax.named_scope("bias"):
        tile = jnp.einsum(
            "jkc,ch->hkj", normed.astype(F32), w_bias, precision=lax.Precision.HIGHEST
        )
        kept = lax.dynamic_slice_in_dim(tile, core * 32, 32, 1)
        sent = lax.dynamic_slice_in_dim(tile, (1 - core) * 32, 32, 1)
        got = move(sent, lambda y, z, core, x: (y, z, 1 - core, x))
        tile = jnp.where(
            core == 0, jnp.concatenate([kept, got], 2), jnp.concatenate([got, kept], 2)
        )
        rounds = []
        for step in range(4):
            part = lax.dynamic_index_in_dim(tile, (x + step) % 4, 0, keepdims=False)
            rounds.append(move(part, lambda y, z, core, x: (x + step, z, core, y)))
        rounds = jnp.stack(rounds + rounds[:3])
        block = lax.dynamic_slice_in_dim(rounds, (y - x) % 4, 4, 0).reshape(128, 128)
        along_z = [block]
        for step in range(1, 8):
            along_z.append(move(block, lambda y, z, core, x: (y, z + step, core, x)))
        along_z = jnp.stack(along_z)
        biases = []
        for step in range(4):
            here = (
                along_z
                if step == 0
                else move(along_z, lambda y, z, core, x: (y + step, z, core, x))
            )
            biases.append((here, move(here, lambda y, z, core, x: (y, z, 1 - core, x))))
    count = 16 // CHUNKS
    result = jnp.zeros(pair.shape, BF)
    for chunk in range(CHUNKS):
        with jax.named_scope("rows"):
            pieces = []
            for step in range(4):
                part = lax.dynamic_slice_in_dim(
                    normed, (zl + step) % 4 * 16 + chunk * count, count, 0
                )
                if step:
                    part = move(part, lambda y, z, core, x: (y, turn(z, step), core, x))
                pieces.append(part)
            held = jnp.stack(pieces)
            rows = [held]
            for step in range(1, 4):
                rows.append(move(held, lambda y, z, core, x: (y, z, core, x + step)))
        with jax.named_scope("attention"):
            part = attend(
                place,
                rows,
                biases,
                w_key,
                w_value.T,
                w_query.T,
                w_gate.T,
                gate_shift[:, None],
                w_out,
                out_shift[None],
            )
        with jax.named_scope("update"):
            for step in range(4):
                back = part[step]
                if step:
                    back = move(back, lambda y, z, core, x: (y, turn(z, -step), core, x))
                result = lax.dynamic_update_slice_in_dim(
                    result, back, (zl + step) % 4 * 16 + chunk * count, 0
                )
    return result


def solution(mesh):
    in_specs = (P("row", "col", None), P(), P(), P(), P(), P(), P(), P(), P(), P(), P())
    out_specs = P("row", "col", None)
    return jax.shard_map(
        on_device, mesh=mesh, in_specs=in_specs, out_specs=out_specs, check_vma=False
    )
```

```python
import functools
import math

import jax
import jax.numpy as jnp
from jax import lax
from jax.experimental import pallas as pl
from jax.experimental.pallas import tpu as pltpu
from jax.sharding import Mesh
from jax.sharding import PartitionSpec as P

F32 = jnp.float32
BF = jnp.bfloat16
CHUNKS = 2
TOGETHER = 2
DEPTH = 32


def dot(a, b):
    return jnp.dot(a, b, preferred_element_type=F32)


def dot_t(a, b):
    return lax.dot_general(a, b, (((1,), (1,)), ((), ())), preferred_element_type=F32)


def fold(function, so_far, value):
    return value if so_far is None else function(so_far, value)


def attend_kernel(
    at,
    rows,
    b00,
    b01,
    b10,
    b11,
    b20,
    b21,
    b30,
    b31,
    w_key,
    w_value_t,
    w_query_t,
    w_gate_t,
    gate_shift,
    w_out,
    out_shift,
    out,
    key_ref,
    value_ref,
    score_ref,
    attended_ref,
):
    bias = ((b00, b01), (b10, b11), (b20, b21), (b30, b31))
    y, x, zl, core = at[0], at[1], at[2], at[3]
    slot = [lax.rem(zl + 4 - part, 4) for part in range(4)]
    heads = [lax.rem(y + 4 - step, 4) for step in range(4)]
    halves = [pl.multiple_of(lax.rem(core + half, 2) * 32, 32) for half in range(2)]
    xs = [lax.rem(x + 4 - step, 4) for step in range(4)]
    kept = [{} for _ in range(TOGETHER)]

    def project_query(r):
        tokens = jnp.concatenate([rows[x, slot[part], r] for part in range(4)], axis=0)
        query = (dot_t(w_query_t[...], tokens) * (1.0 / math.sqrt(DEPTH))).astype(BF)
        gate = jax.nn.sigmoid(dot_t(w_gate_t[...], tokens) + gate_shift[...])
        of_head = lax.broadcasted_iota(jnp.int32, query.shape, 0) // DEPTH
        zero = jnp.zeros_like(query)
        return [jnp.where(of_head == head, query, zero) for head in heads], gate

    def project(r):
        tokens = jnp.concatenate(
            [
                rows[xs[t], s, r, pl.ds(halves[half], 32), :]
                for half in range(2)
                for s in range(4)
                for t in range(4)
            ],
            axis=0,
        )
        key_ref[r] = dot(tokens, w_key[...]).astype(BF)
        value_ref[r] = dot_t(w_value_t[...], tokens).astype(BF)
        kept[r]["query"], kept[r]["gate"] = project_query(r)

    def score(r, a, c, query):
        half, s = divmod(c, 4)
        z_of = [zh * 4 + lax.rem(zl + 4 - s, 4) for zh in range(2)]
        added = jnp.concatenate([bias[a][half][z] for z in z_of], axis=1)
        return dot(key_ref[r, c * 128 : (c + 1) * 128, :], query[a]) + added

    def raise_plain(r, a):
        total = None
        for c in range(8):
            raised = jnp.exp(score(r, a, c, kept[r]["query"]))
            score_ref[r, a, c] = raised
            total = fold(jnp.add, total, jnp.sum(raised.reshape(16, 8, 256), axis=0))
        return jnp.sum(total, axis=0, keepdims=True)

    def raise_shifted(r, a, query):
        largest = None
        for c in range(8):
            scores = score(r, a, c, query)
            score_ref[r, a, c] = scores
            largest = fold(
                jnp.maximum, largest, jnp.max(scores.reshape(16, 8, 256), axis=0)
            )
        largest = jnp.max(largest, axis=0, keepdims=True)
        total = None
        for c in range(8):
            raised = jnp.exp(score_ref[r, a, c] - largest)
            score_ref[r, a, c] = raised
            total = fold(jnp.add, total, jnp.sum(raised.reshape(16, 8, 256), axis=0))
        return jnp.sum(total, axis=0, keepdims=True)

    def weigh(r, a, total):
        scale = 1.0 / total
        weights = jnp.concatenate(
            [(score_ref[r, a, c] * scale).astype(BF) for c in range(8)], axis=0
        )
        own = pl.ds(pl.multiple_of(heads[a] * DEPTH, DEPTH), DEPTH)
        attended_ref[r, own, :] = dot(value_ref[r, own, :], weights)

    def finish(r, gate):
        gated = (gate * attended_ref[r]).astype(BF)
        update = lax.dot_general(
            gated, w_out[...], (((0,), (0,)), ((), ())), preferred_element_type=F32
        )
        update = (update + out_shift[...]).astype(BF)
        for part in range(4):
            out[slot[part], r] = update[part * 64 : (part + 1) * 64]

    for r in range(TOGETHER):
        project(r)
    totals = {}
    for r in range(TOGETHER):
        for a in range(4):
            totals[r, a] = raise_plain(r, a)
    for r in range(TOGETHER):
        for a in range(4):
            weigh(r, a, totals[r, a])
    for r in range(TOGETHER):
        finish(r, kept[r]["gate"])

    safe = None
    for total in totals.values():
        inside = jnp.logical_and(total > 2.0**-60, total < 2.0**120)
        safe = fold(jnp.minimum, safe, jnp.where(inside, 1.0, 0.0))

    @pl.when(jnp.min(safe) < 0.5)
    def _():
        for r in range(TOGETHER):
            query, gate = project_query(r)
            for a in range(4):
                weigh(r, a, raise_shifted(r, a, query))
            finish(r, gate)


def attend(at, rows, biases, *weights):
    count = rows.shape[2]
    whole = lambda a: pl.BlockSpec(a.shape, lambda i, at: (0,) * a.ndim)
    biases = [b for pair in biases for b in pair]
    return pl.pallas_call(
        attend_kernel,
        out_shape=jax.ShapeDtypeStruct((4, count, 64, 128), BF),
        grid_spec=pltpu.PrefetchScalarGridSpec(
            num_scalar_prefetch=1,
            grid=(count // TOGETHER,),
            in_specs=[
                pl.BlockSpec((4, 4, TOGETHER, 64, 128), lambda i, at: (0, 0, i, 0, 0))
            ]
            + [whole(a) for a in biases]
            + [whole(a) for a in weights],
            out_specs=pl.BlockSpec((4, TOGETHER, 64, 128), lambda i, at: (0, i, 0, 0)),
            scratch_shapes=[
                pltpu.VMEM((TOGETHER, 1024, 128), BF),
                pltpu.VMEM((TOGETHER, 128, 1024), BF),
                pltpu.VMEM((TOGETHER, 4, 8, 128, 256), F32),
                pltpu.VMEM((TOGETHER, 128, 256), F32),
            ],
        ),
        compiler_params=pltpu.CompilerParams(
            vmem_limit_bytes=48 << 20, dimension_semantics=("arbitrary",)
        ),
        cost_estimate=pl.CostEstimate(
            flops=count * 300_000_000,
            bytes_accessed=count << 20,
            transcendentals=count << 20,
        ),
    )(at, rows, *biases, *weights)


def normalize(values, gain, shift):
    values = values.astype(F32)
    mean = jnp.mean(values, axis=-1, keepdims=True)
    centred = values - mean
    spread = jnp.mean(centred * centred, axis=-1, keepdims=True)
    return (centred * lax.rsqrt(spread + 1e-05) * gain + shift).astype(BF)


def stack_kernel(*refs):
    *pieces, _, out = refs
    for at, piece in enumerate(pieces):
        out[at] = piece[...]


def stack_after(pieces, after):
    return pl.pallas_call(
        stack_kernel,
        out_shape=jax.ShapeDtypeStruct((len(pieces), *pieces[0].shape), BF),
        in_specs=[pl.BlockSpec(memory_space=pltpu.VMEM)] * len(pieces)
        + [pl.BlockSpec(memory_space=pl.ANY)],
        out_specs=pl.BlockSpec(memory_space=pltpu.VMEM),
        name="stack_rows",
    )(*pieces, after)


AXES = ("y", "zh", "core", "x", "zl")


def move(array, to):
    pairs = []
    for source in range(256):
        row, col = divmod(source, 16)
        y, zh, core = row // 4, row // 2 % 2, row % 2
        x, zl = divmod(col, 4)
        y, z, core, x = to(y, zh * 4 + zl, core, x)
        y, z, x = y % 4, z % 8, x % 4
        target = ((y * 2 + z // 4) * 2 + core) * 16 + x * 4 + z % 4
        pairs.append((source, target))
    return lax.ppermute(array, AXES, pairs)


def swap_cores(array):
    return move(array, lambda y, z, core, x: (y, z, 1 - core, x))


def turn(z, step):
    return z // 4 * 4 + (z + step) % 4


def on_device(
    pair,
    norm_gain,
    norm_shift,
    w_query,
    w_key,
    w_value,
    w_gate,
    gate_shift,
    w_bias,
    w_out,
    out_shift,
):
    y, core, x, zl = (lax.axis_index(name) for name in ("y", "core", "x", "zl"))
    place = jnp.stack([y, x, zl, core]).astype(jnp.int32)
    normed = normalize(pair, norm_gain, norm_shift)
    count = 16 // CHUNKS

    def exchange(normed, chunk, after):
        with jax.named_scope("rows"):
            pieces = []
            for step in range(4):
                part = lax.dynamic_slice_in_dim(
                    normed, (zl + step) % 4 * 16 + chunk * count, count, 0
                )
                if step:
                    part = move(part, lambda y, z, core, x: (y, turn(z, step), core, x))
                pieces.append(part)
            held = stack_after(pieces, after)
            return lax.all_gather(held, "x", axis=0, tiled=False)

    with jax.named_scope("bias"):
        tile = jnp.einsum(
            "jkc,ch->hkj", normed.astype(F32), w_bias, precision=lax.Precision.HIGHEST
        )
        kept = lax.dynamic_slice_in_dim(tile, core * 32, 32, 1)
        sent = lax.dynamic_slice_in_dim(tile, (1 - core) * 32, 32, 1)
        kept, sent, normed = lax.optimization_barrier((kept, sent, normed))
        got = swap_cores(sent)
        normed0 = normed
        tile = jnp.where(
            core == 0, jnp.concatenate([kept, got], 2), jnp.concatenate([got, kept], 2)
        )
        rounds = []
        for step in range(4):
            part = lax.dynamic_index_in_dim(tile, (x + step) % 4, 0, keepdims=False)
            rounds.append(move(part, lambda y, z, core, x: (x + step, z, core, y)))
        rounds = jnp.stack(rounds + rounds[:3])
        block = lax.dynamic_slice_in_dim(rounds, (y - x) % 4, 4, 0).reshape(128, 128)
        block, normed = lax.optimization_barrier((block, normed))
        along_z = lax.all_to_all(
            jnp.broadcast_to(block[None], (8, 128, 128)),
            ("zh", "zl"),
            split_axis=0,
            concat_axis=0,
            tiled=True,
        )
    rows = [exchange(normed0, 0, block)]
    with jax.named_scope("bias"):
        biases = []
        for step in range(4):
            here = along_z
            if step:
                here = move(along_z, lambda y, z, core, x: (y + step, z, core, x))
            biases.append((here, swap_cores(here)))
    for chunk in range(1, CHUNKS):
        rows.append(exchange(normed, chunk, along_z))
    result = jnp.zeros(pair.shape, BF)
    for chunk in range(CHUNKS):
        with jax.named_scope("attention"):
            part = attend(
                place,
                rows[chunk],
                biases,
                w_key,
                w_value.T,
                w_query.T,
                w_gate.T,
                gate_shift[:, None],
                w_out,
                out_shift[None],
            )
        with jax.named_scope("update"):
            for step in range(4):
                back = part[step]
                if step:
                    back = move(back, lambda y, z, core, x: (y, turn(z, -step), core, x))
                result = lax.dynamic_update_slice_in_dim(
                    result, back, (zl + step) % 4 * 16 + chunk * count, 0
                )
    return result


def solution(mesh):
    parts = Mesh(mesh.devices.reshape(4, 2, 2, 4, 4), AXES)
    tiles = P(("y", "zh", "core"), ("x", "zl"), None)
    return jax.shard_map(
        on_device,
        mesh=parts,
        in_specs=(tiles,) + (P(),) * 10,
        out_specs=tiles,
        check_vma=False,
    )
```

```python
import functools
import math

import jax
import jax.numpy as jnp
from jax import lax
from jax.experimental import pallas as pl
from jax.experimental.pallas import tpu as pltpu
from jax.sharding import Mesh
from jax.sharding import PartitionSpec as P

F32 = jnp.float32
BF = jnp.bfloat16
CHUNKS = ((0, 12), (12, 4))
TOGETHER = 2
DEPTH = 32


def dot(a, b):
    return jnp.dot(a, b, preferred_element_type=F32)


def dot_t(a, b):
    return lax.dot_general(a, b, (((1,), (1,)), ((), ())), preferred_element_type=F32)


def fold(function, so_far, value):
    return value if so_far is None else function(so_far, value)


def attend_kernel(
    at,
    rows,
    b00,
    b01,
    b10,
    b11,
    b20,
    b21,
    b30,
    b31,
    w_key,
    w_value_t,
    w_query_t,
    w_gate_t,
    gate_shift,
    w_out,
    out_shift,
    out,
    key_ref,
    value_ref,
    score_ref,
    attended_ref,
):
    bias = ((b00, b01), (b10, b11), (b20, b21), (b30, b31))
    y, x, zl, core = at[0], at[1], at[2], at[3]
    slot = [lax.rem(zl + 4 - part, 4) for part in range(4)]
    heads = [lax.rem(y + 4 - step, 4) for step in range(4)]
    halves = [pl.multiple_of(lax.rem(core + half, 2) * 32, 32) for half in range(2)]
    xs = [lax.rem(x + 4 - step, 4) for step in range(4)]
    kept = [{} for _ in range(TOGETHER)]

    def project_query(r):
        tokens = jnp.concatenate([rows[x, slot[part], r] for part in range(4)], axis=0)
        query = (dot_t(w_query_t[...], tokens) * (1.0 / math.sqrt(DEPTH))).astype(BF)
        gate = jax.nn.sigmoid(dot_t(w_gate_t[...], tokens) + gate_shift[...])
        of_head = lax.broadcasted_iota(jnp.int32, query.shape, 0) // DEPTH
        zero = jnp.zeros_like(query)
        return [jnp.where(of_head == head, query, zero) for head in heads], gate

    def project(r):
        tokens = jnp.concatenate(
            [
                rows[xs[t], s, r, pl.ds(halves[half], 32), :]
                for half in range(2)
                for s in range(4)
                for t in range(4)
            ],
            axis=0,
        )
        key_ref[r] = dot(tokens, w_key[...]).astype(BF)
        value_ref[r] = dot_t(w_value_t[...], tokens).astype(BF)
        kept[r]["query"], kept[r]["gate"] = project_query(r)

    def score(r, a, c, query):
        half, s = divmod(c, 4)
        z_of = [zh * 4 + lax.rem(zl + 4 - s, 4) for zh in range(2)]
        added = jnp.concatenate([bias[a][half][z] for z in z_of], axis=1)
        return dot(key_ref[r, c * 128 : (c + 1) * 128, :], query[a]) + added

    def raise_plain(r, a):
        total = None
        for c in range(8):
            raised = jnp.exp(score(r, a, c, kept[r]["query"]))
            score_ref[r, a, c] = raised
            total = fold(jnp.add, total, jnp.sum(raised.reshape(16, 8, 256), axis=0))
        return jnp.sum(total, axis=0, keepdims=True)

    def raise_shifted(r, a, query):
        largest = None
        for c in range(8):
            scores = score(r, a, c, query)
            score_ref[r, a, c] = scores
            largest = fold(
                jnp.maximum, largest, jnp.max(scores.reshape(16, 8, 256), axis=0)
            )
        largest = jnp.max(largest, axis=0, keepdims=True)
        total = None
        for c in range(8):
            raised = jnp.exp(score_ref[r, a, c] - largest)
            score_ref[r, a, c] = raised
            total = fold(jnp.add, total, jnp.sum(raised.reshape(16, 8, 256), axis=0))
        return jnp.sum(total, axis=0, keepdims=True)

    def weigh(r, a, total):
        scale = 1.0 / total
        weights = jnp.concatenate(
            [(score_ref[r, a, c] * scale).astype(BF) for c in range(8)], axis=0
        )
        own = pl.ds(pl.multiple_of(heads[a] * DEPTH, DEPTH), DEPTH)
        attended_ref[r, own, :] = dot(value_ref[r, own, :], weights)

    def finish(r, gate):
        gated = (gate * attended_ref[r]).astype(BF)
        update = lax.dot_general(
            gated, w_out[...], (((0,), (0,)), ((), ())), preferred_element_type=F32
        )
        update = (update + out_shift[...]).astype(BF)
        for part in range(4):
            out[slot[part], r] = update[part * 64 : (part + 1) * 64]

    for r in range(TOGETHER):
        project(r)
    totals = {}
    for r in range(TOGETHER):
        for a in range(4):
            totals[r, a] = raise_plain(r, a)
    for r in range(TOGETHER):
        for a in range(4):
            weigh(r, a, totals[r, a])
    for r in range(TOGETHER):
        finish(r, kept[r]["gate"])

    safe = None
    for total in totals.values():
        inside = jnp.logical_and(total > 2.0**-60, total < 2.0**120)
        safe = fold(jnp.minimum, safe, jnp.where(inside, 1.0, 0.0))

    @pl.when(jnp.min(safe) < 0.5)
    def _():
        for r in range(TOGETHER):
            query, gate = project_query(r)
            for a in range(4):
                weigh(r, a, raise_shifted(r, a, query))
            finish(r, gate)


def attend(at, rows, biases, *weights):
    count = rows.shape[2]
    whole = lambda a: pl.BlockSpec(a.shape, lambda i, at: (0,) * a.ndim)
    biases = [b for pair in biases for b in pair]
    return pl.pallas_call(
        attend_kernel,
        out_shape=jax.ShapeDtypeStruct((4, count, 64, 128), BF),
        grid_spec=pltpu.PrefetchScalarGridSpec(
            num_scalar_prefetch=1,
            grid=(count // TOGETHER,),
            in_specs=[
                pl.BlockSpec((4, 4, TOGETHER, 64, 128), lambda i, at: (0, 0, i, 0, 0))
            ]
            + [whole(a) for a in biases]
            + [whole(a) for a in weights],
            out_specs=pl.BlockSpec((4, TOGETHER, 64, 128), lambda i, at: (0, i, 0, 0)),
            scratch_shapes=[
                pltpu.VMEM((TOGETHER, 1024, 128), BF),
                pltpu.VMEM((TOGETHER, 128, 1024), BF),
                pltpu.VMEM((TOGETHER, 4, 8, 128, 256), F32),
                pltpu.VMEM((TOGETHER, 128, 256), F32),
            ],
        ),
        compiler_params=pltpu.CompilerParams(
            vmem_limit_bytes=48 << 20, dimension_semantics=("arbitrary",)
        ),
        cost_estimate=pl.CostEstimate(
            flops=count * 300_000_000,
            bytes_accessed=count << 20,
            transcendentals=count << 20,
        ),
    )(at, rows, *biases, *weights)


def normalize(values, gain, shift):
    values = values.astype(F32)
    mean = jnp.mean(values, axis=-1, keepdims=True)
    centred = values - mean
    spread = jnp.mean(centred * centred, axis=-1, keepdims=True)
    return (centred * lax.rsqrt(spread + 1e-05) * gain + shift).astype(BF)


def stack_kernel(*refs):
    *pieces, _, out = refs
    for at, piece in enumerate(pieces):
        out[at] = piece[...]


def stack_after(pieces, after):
    return pl.pallas_call(
        stack_kernel,
        out_shape=jax.ShapeDtypeStruct((len(pieces), *pieces[0].shape), BF),
        in_specs=[pl.BlockSpec(memory_space=pltpu.VMEM)] * len(pieces)
        + [pl.BlockSpec(memory_space=pl.ANY)],
        out_specs=pl.BlockSpec(memory_space=pltpu.VMEM),
        name="stack_rows",
    )(*pieces, after)


def assemble_kernel(at, *refs):
    *blocks, out = refs
    for i, block in enumerate(blocks):
        chunk, step = divmod(i, 4)
        start = lax.rem(at[2] + step, 4) * 16 + CHUNKS[chunk][0]
        out[pl.ds(start, CHUNKS[chunk][1])] = block[...]


def assemble(at, blocks):
    return pl.pallas_call(
        assemble_kernel,
        out_shape=jax.ShapeDtypeStruct((64, 64, 128), BF),
        in_specs=[pl.BlockSpec(memory_space=pltpu.SMEM)]
        + [pl.BlockSpec(memory_space=pltpu.VMEM)] * len(blocks),
        out_specs=pl.BlockSpec(memory_space=pltpu.VMEM),
        name="assemble_update",
    )(at, *blocks)


AXES = ("y", "zh", "core", "x", "zl")


def move(array, to):
    pairs = []
    for source in range(256):
        row, col = divmod(source, 16)
        y, zh, core = row // 4, row // 2 % 2, row % 2
        x, zl = divmod(col, 4)
        y, z, core, x = to(y, zh * 4 + zl, core, x)
        y, z, x = y % 4, z % 8, x % 4
        target = ((y * 2 + z // 4) * 2 + core) * 16 + x * 4 + z % 4
        pairs.append((source, target))
    return lax.ppermute(array, AXES, pairs)


def swap_cores(array):
    return move(array, lambda y, z, core, x: (y, z, 1 - core, x))


def turn(z, step):
    return z // 4 * 4 + (z + step) % 4


def on_device(
    pair,
    norm_gain,
    norm_shift,
    w_query,
    w_key,
    w_value,
    w_gate,
    gate_shift,
    w_bias,
    w_out,
    out_shift,
):
    y, core, x, zl = (lax.axis_index(name) for name in ("y", "core", "x", "zl"))
    place = jnp.stack([y, x, zl, core]).astype(jnp.int32)
    normed = normalize(pair, norm_gain, norm_shift)
    def exchange(normed, chunk, after):
        with jax.named_scope("rows"):
            pieces = []
            for step in range(4):
                part = lax.dynamic_slice_in_dim(
                    normed, (zl + step) % 4 * 16 + CHUNKS[chunk][0], CHUNKS[chunk][1], 0
                )
                if step:
                    part = move(part, lambda y, z, core, x: (y, turn(z, step), core, x))
                pieces.append(part)
            held = stack_after(pieces, after)
            return lax.all_gather(held, "x", axis=0, tiled=False)

    with jax.named_scope("bias"):
        tile = jnp.einsum(
            "jkc,ch->hkj", normed.astype(F32), w_bias, precision=lax.Precision.HIGHEST
        )
        kept = lax.dynamic_slice_in_dim(tile, core * 32, 32, 1)
        sent = lax.dynamic_slice_in_dim(tile, (1 - core) * 32, 32, 1)
        got = swap_cores(sent)
        tile = jnp.where(
            core == 0, jnp.concatenate([kept, got], 2), jnp.concatenate([got, kept], 2)
        )
        rounds = []
        for step in range(4):
            part = lax.dynamic_index_in_dim(tile, (x + step) % 4, 0, keepdims=False)
            rounds.append(move(part, lambda y, z, core, x: (x + step, z, core, y)))
        rounds = jnp.stack(rounds + rounds[:3])
        block = lax.dynamic_slice_in_dim(rounds, (y - x) % 4, 4, 0).reshape(128, 128)
        along_z = lax.all_to_all(
            jnp.broadcast_to(block[None], (8, 128, 128)),
            ("zh", "zl"),
            split_axis=0,
            concat_axis=0,
            tiled=True,
        )
    rows = [exchange(normed, 0, block)]
    with jax.named_scope("bias"):
        biases = []
        for step in range(4):
            here = along_z
            if step:
                here = move(along_z, lambda y, z, core, x: (y + step, z, core, x))
            biases.append((here, swap_cores(here)))
    for chunk in range(1, len(CHUNKS)):
        rows.append(exchange(normed, chunk, along_z))
    blocks = []
    for chunk in range(len(CHUNKS)):
        with jax.named_scope("attention"):
            part = attend(
                place,
                rows[chunk],
                biases,
                w_key,
                w_value.T,
                w_query.T,
                w_gate.T,
                gate_shift[:, None],
                w_out,
                out_shift[None],
            )
        with jax.named_scope("update"):
            for step in range(4):
                back = part[step]
                if step:
                    back = move(back, lambda y, z, core, x: (y, turn(z, -step), core, x))
                blocks.append(back)
    return assemble(place, blocks)


def solution(mesh):
    parts = Mesh(mesh.devices.reshape(4, 2, 2, 4, 4), AXES)
    tiles = P(("y", "zh", "core"), ("x", "zl"), None)
    return jax.shard_map(
        on_device,
        mesh=parts,
        in_specs=(tiles,) + (P(),) * 10,
        out_specs=tiles,
        check_vma=False,
    )
```

```python
import functools
import math

import jax
import jax.numpy as jnp
from jax import lax
from jax.experimental import pallas as pl
from jax.experimental.pallas import tpu as pltpu
from jax.sharding import Mesh
from jax.sharding import PartitionSpec as P

F32 = jnp.float32
BF = jnp.bfloat16
TOGETHER = 2
DEPTH = 32


def dot(a, b):
    return jnp.dot(a, b, preferred_element_type=F32)


def dot_t(a, b):
    return lax.dot_general(a, b, (((1,), (1,)), ((), ())), preferred_element_type=F32)


def fold(function, so_far, value):
    return value if so_far is None else function(so_far, value)


def places(at):
    y, x, zl, core = at[0], at[1], at[2], at[3]
    slot = [lax.rem(zl + 4 - part, 4) for part in range(4)]
    halves = [pl.multiple_of(lax.rem(core + half, 2) * 32, 32) for half in range(2)]
    z_of = [[zh * 4 + lax.rem(zl + 4 - s, 4) for zh in range(2)] for s in range(4)]
    return y, slot, halves, z_of


def attend_heads(heads, bias, z_of, key, query, value, put, score_ref):
    work = [(r, a) for r in range(TOGETHER) for a in range(len(heads))]

    def masked(r, a):
        of_head = lax.broadcasted_iota(jnp.int32, (128, 256), 0) // DEPTH
        read = query(r)
        return jnp.where(of_head == heads[a], read, jnp.zeros_like(read))

    def score(r, a, c, own):
        half, s = divmod(c, 4)
        added = jnp.concatenate([bias(a, half, z) for z in z_of[s]], axis=1)
        return dot(key(r, c), own) + added

    def raise_plain(r, a):
        own, total = masked(r, a), None
        for c in range(8):
            raised = jnp.exp(score(r, a, c, own))
            score_ref[r, a, c] = raised
            total = fold(jnp.add, total, jnp.sum(raised.reshape(16, 8, 256), axis=0))
        return jnp.sum(total, axis=0, keepdims=True)

    def raise_shifted(r, a):
        own, largest, total = masked(r, a), None, None
        for c in range(8):
            scores = score(r, a, c, own)
            score_ref[r, a, c] = scores
            top = jnp.max(scores.reshape(16, 8, 256), axis=0)
            largest = fold(jnp.maximum, largest, top)
        largest = jnp.max(largest, axis=0, keepdims=True)
        for c in range(8):
            raised = jnp.exp(score_ref[r, a, c] - largest)
            score_ref[r, a, c] = raised
            total = fold(jnp.add, total, jnp.sum(raised.reshape(16, 8, 256), axis=0))
        return jnp.sum(total, axis=0, keepdims=True)

    def weigh(r, a, total):
        scale = 1.0 / total
        weights = jnp.concatenate(
            [(score_ref[r, a, c] * scale).astype(BF) for c in range(8)], axis=0
        )
        own = pl.ds(pl.multiple_of(heads[a] * DEPTH, DEPTH), DEPTH)
        put(r, own, dot(value(r, own), weights))

    totals = [raise_plain(r, a) for r, a in work]
    for (r, a), total in zip(work, totals):
        weigh(r, a, total)

    safe = None
    for total in totals:
        inside = jnp.logical_and(total > 2.0**-60, total < 2.0**120)
        safe = fold(jnp.minimum, safe, jnp.where(inside, 1.0, 0.0))

    def again():
        for r, a in work:
            weigh(r, a, raise_shifted(r, a))

    return jnp.min(safe) < 0.5, again


def first_kernel(
    at,
    x0,
    x1,
    x2,
    x3,
    bias_own,
    bias_other,
    w_key,
    w_value_t,
    w_query_t,
    w_gate_t,
    gate_shift,
    key_out,
    value_out,
    query_out,
    gate_out,
    attended_out,
    score_ref,
):
    rows, bias = (x0, x1, x2, x3), (bias_own, bias_other)
    y, slot, halves, z_of = places(at)
    for r in range(TOGETHER):
        tokens = jnp.concatenate(
            [
                rows[t][s, r, pl.ds(halves[half], 32), :]
                for half in range(2)
                for s in range(4)
                for t in range(4)
            ],
            axis=0,
        )
        key_out[r] = dot(tokens, w_key[...]).astype(BF)
        value_out[r] = dot_t(w_value_t[...], tokens).astype(BF)
        tokens = jnp.concatenate([x0[slot[part], r] for part in range(4)], axis=0)
        query = dot_t(w_query_t[...], tokens) * (1.0 / math.sqrt(DEPTH))
        query_out[r] = query.astype(BF)
        gate_out[r] = jax.nn.sigmoid(dot_t(w_gate_t[...], tokens) + gate_shift[...])

    def put(r, own, attended):
        attended_out[r] = attended

    unsafe, again = attend_heads(
        [y],
        lambda a, half, z: bias[half][z],
        z_of,
        lambda r, c: key_out[r, c * 128 : (c + 1) * 128, :],
        lambda r: query_out[r],
        lambda r, own: value_out[r, own, :],
        put,
        score_ref,
    )
    pl.when(unsafe)(again)


def second_kernel(
    at,
    key,
    value,
    query,
    gate,
    attended,
    bias_own,
    bias_other,
    w_out,
    out_shift,
    out,
    attended_ref,
    score_ref,
):
    bias = (bias_own, bias_other)
    y, slot, _, z_of = places(at)
    heads = [lax.rem(y + step, 4) for step in range(1, 4)]
    own = pl.ds(pl.multiple_of(y * DEPTH, DEPTH), DEPTH)
    for r in range(TOGETHER):
        attended_ref[r, own, :] = attended[r]

    def put(r, own, attended):
        attended_ref[r, own, :] = attended

    def finish():
        for r in range(TOGETHER):
            gated = (gate[r] * attended_ref[r]).astype(BF)
            update = lax.dot_general(
                gated, w_out[...], (((0,), (0,)), ((), ())), preferred_element_type=F32
            )
            update = (update + out_shift[...]).astype(BF)
            for part in range(4):
                out[slot[part], r] = update[part * 64 : (part + 1) * 64]

    unsafe, again = attend_heads(
        heads,
        lambda a, half, z: bias[half][heads[a], z],
        z_of,
        lambda r, c: key[r, c * 128 : (c + 1) * 128, :],
        lambda r: query[r],
        lambda r, own: value[r, own, :],
        put,
        score_ref,
    )
    finish()

    @pl.when(unsafe)
    def _():
        again()
        finish()


def call(kernel, name, count, at, operands, outs, scratch, work):
    def spec(shape, dim, first=0):
        if dim is None:
            return pl.BlockSpec(shape, lambda i, at: (0,) * len(shape))
        block = shape[:dim] + (TOGETHER,) + shape[dim + 1 :]
        where = (0,) * dim, (0,) * (len(shape) - dim - 1)
        return pl.BlockSpec(block, lambda i, at: where[0] + (i + first,) + where[1])

    return pl.pallas_call(
        kernel,
        out_shape=[jax.ShapeDtypeStruct(shape, dtype) for shape, dtype, _ in outs],
        grid_spec=pltpu.PrefetchScalarGridSpec(
            num_scalar_prefetch=1,
            grid=(count // TOGETHER,),
            in_specs=[spec(array.shape, *rest) for array, *rest in operands],
            out_specs=[spec(shape, dim) for shape, _, dim in outs],
            scratch_shapes=scratch,
        ),
        compiler_params=pltpu.CompilerParams(
            vmem_limit_bytes=48 << 20, dimension_semantics=("arbitrary",)
        ),
        cost_estimate=pl.CostEstimate(
            flops=count * 300_000_000,
            bytes_accessed=count << 20,
            transcendentals=count * work,
        ),
        name=name,
    )(at, *[array for array, *_ in operands])


def attend_first(at, rows, first, bias, weights):
    count = 8
    operands = [(array, 1, start // TOGETHER) for array, start in zip(rows, first)]
    operands += [(array, None) for array in (*bias, *weights)]
    outs = [
        ((count, 1024, 128), BF, 0),
        ((count, 128, 1024), BF, 0),
        ((count, 128, 256), BF, 0),
        ((count, 128, 256), F32, 0),
        ((count, 32, 256), F32, 0),
    ]
    scratch = [pltpu.VMEM((TOGETHER, 1, 8, 128, 256), F32)]
    return call(
        first_kernel, "project_own_head", count, at, operands, outs, scratch, 1 << 18
    )


def attend_second(at, held, bias, weights):
    count = 8
    operands = [(array, 0) for array in held]
    operands += [(array, None) for array in (*bias, *weights)]
    outs = [((4, count, 64, 128), BF, 1)]
    scratch = [
        pltpu.VMEM((TOGETHER, 128, 256), F32),
        pltpu.VMEM((TOGETHER, 3, 8, 128, 256), F32),
    ]
    return call(
        second_kernel, "other_heads", count, at, operands, outs, scratch, 3 << 18
    )[0]


def normalize(values, gain, shift):
    values = values.astype(F32)
    mean = jnp.mean(values, axis=-1, keepdims=True)
    centred = values - mean
    spread = jnp.mean(centred * centred, axis=-1, keepdims=True)
    return (centred * lax.rsqrt(spread + 1e-05) * gain + shift).astype(BF)


def assemble_kernel(at, *refs):
    *blocks, out = refs
    count = blocks[0].shape[0]
    for i, block in enumerate(blocks):
        chunk, step = divmod(i, 4)
        start = lax.rem(at[2] + step, 4) * 16 + chunk * count
        out[pl.ds(start, count)] = block[...]


def assemble(at, blocks):
    return pl.pallas_call(
        assemble_kernel,
        out_shape=jax.ShapeDtypeStruct((64, 64, 128), BF),
        in_specs=[pl.BlockSpec(memory_space=pltpu.SMEM)]
        + [pl.BlockSpec(memory_space=pltpu.VMEM)] * len(blocks),
        out_specs=pl.BlockSpec(memory_space=pltpu.VMEM),
        name="assemble_update",
    )(at, *blocks)


def tie_kernel(array, *rest):
    pass


def after(array, *earlier):
    return pl.pallas_call(
        tie_kernel,
        out_shape=jax.ShapeDtypeStruct(array.shape, array.dtype),
        in_specs=[pl.BlockSpec(memory_space=pl.ANY)] * (1 + len(earlier)),
        out_specs=pl.BlockSpec(memory_space=pl.ANY),
        input_output_aliases={0: 0},
        name="tie",
    )(array, *earlier)


AXES = ("y", "zh", "core", "x", "zl")


def move(array, to):
    pairs = []
    for source in range(256):
        row, col = divmod(source, 16)
        y, zh, core = row // 4, row // 2 % 2, row % 2
        x, zl = divmod(col, 4)
        y, z, core, x = to(y, zh * 4 + zl, core, x)
        y, z, x = y % 4, z % 8, x % 4
        target = ((y * 2 + z // 4) * 2 + core) * 16 + x * 4 + z % 4
        pairs.append((source, target))
    return lax.ppermute(array, AXES, pairs)


def swap_cores(array):
    return move(array, lambda y, z, core, x: (y, z, 1 - core, x))


def turn(z, step):
    return z // 4 * 4 + (z + step) % 4


def on_device(
    pair,
    norm_gain,
    norm_shift,
    w_query,
    w_key,
    w_value,
    w_gate,
    gate_shift,
    w_bias,
    w_out,
    out_shift,
):
    y, core, x, zl = (lax.axis_index(name) for name in ("y", "core", "x", "zl"))
    place = jnp.stack([y, x, zl, core]).astype(jnp.int32)
    normed = normalize(pair, norm_gain, norm_shift)
    with jax.named_scope("rows"):
        pieces = []
        for step in range(4):
            part = lax.dynamic_slice_in_dim(normed, (zl + step) % 4 * 16, 16, 0)
            if step:
                part = move(part, lambda y, z, core, x: (y, turn(z, step), core, x))
            pieces.append(part)
        here = jnp.stack(pieces)
        below = move(here, lambda y, z, core, x: (y, z, core, x + 1))
        above = move(here, lambda y, z, core, x: (y, z, core, x - 1))
        across = [
            move(below[:, :8], lambda y, z, core, x: (y, z, core, x + 1)),
            move(above[:, 8:], lambda y, z, core, x: (y, z, core, x - 1)),
        ]
        across[0] = after(across[0], across[1])
    with jax.named_scope("bias"):
        tile = jnp.einsum(
            "jkc,ch->hkj", normed.astype(F32), w_bias, precision=lax.Precision.HIGHEST
        )
        kept = lax.dynamic_slice_in_dim(tile, core * 32, 32, 1)
        got = swap_cores(lax.dynamic_slice_in_dim(tile, (1 - core) * 32, 32, 1))
        tile = jnp.where(
            core == 0, jnp.concatenate([kept, got], 2), jnp.concatenate([got, kept], 2)
        )
        rounds = []
        for step in range(4):
            part = lax.dynamic_index_in_dim(tile, (x + step) % 4, 0, keepdims=False)
            rounds.append(move(part, lambda y, z, core, x: (x + step, z, core, y)))
        rounds = jnp.stack(rounds + rounds[:3])
        block = lax.dynamic_slice_in_dim(rounds, (y - x) % 4, 4, 0).reshape(128, 128)
        block = after(block, here)
        along_z = lax.all_to_all(
            jnp.broadcast_to(block[None], (8, 128, 128)),
            ("zh", "zl"),
            split_axis=0,
            concat_axis=0,
            tiled=True,
        )
        own_bias = along_z, swap_cores(along_z)
        whole = lax.all_gather(along_z, "y", axis=0, tiled=False)
    params = (w_key, w_value.T, w_query.T, w_gate.T, gate_shift[:, None])
    blocks = []
    with jax.named_scope("attention"):
        held = [
            attend_first(
                place,
                (here, below, across[chunk], above),
                (8 * chunk, 8 * chunk, 0, 8 * chunk),
                own_bias,
                params,
            )
            for chunk in range(2)
        ]
    with jax.named_scope("bias"):
        whole = after(whole, held[0][4])
        biases = whole, swap_cores(whole)
    for chunk in range(2):
        with jax.named_scope("attention"):
            part = attend_second(place, held[chunk], biases, (w_out, out_shift[None]))
        with jax.named_scope("update"):
            for step in range(4):
                back = part[step]
                if step:
                    back = move(back, lambda y, z, core, x: (y, turn(z, -step), core, x))
                blocks.append(back)
    return assemble(place, blocks)


def solution(mesh):
    parts = Mesh(mesh.devices.reshape(4, 2, 2, 4, 4), AXES)
    tiles = P(("y", "zh", "core"), ("x", "zl"), None)
    return jax.shard_map(
        on_device,
        mesh=parts,
        in_specs=(tiles,) + (P(),) * 10,
        out_specs=tiles,
        check_vma=False,
    )
```

```python
import functools
import math

import jax
import jax.numpy as jnp
from jax import lax
from jax.experimental import pallas as pl
from jax.experimental.pallas import tpu as pltpu
from jax.sharding import Mesh
from jax.sharding import PartitionSpec as P

F32 = jnp.float32
BF = jnp.bfloat16
CHUNKS = 2
TOGETHER = 2
DEPTH = 32


def dot(a, b):
    return jnp.dot(a, b, preferred_element_type=F32)


def dot_t(a, b):
    return lax.dot_general(a, b, (((1,), (1,)), ((), ())), preferred_element_type=F32)


def fold(function, so_far, value):
    return value if so_far is None else function(so_far, value)


def attend_kernel(
    at,
    x0,
    x1,
    x2,
    x3,
    b00,
    b01,
    b10,
    b11,
    b20_low,
    b21_low,
    b20_high,
    b21_high,
    b30,
    b31,
    w_key,
    w_value_t,
    w_query_t,
    w_gate_t,
    gate_shift,
    w_out,
    out_shift,
    out,
    key_ref,
    value_ref,
    score_ref,
    attended_ref,
):
    rows = (x0, x1, x2, x3)
    bias = ((b00, b01), (b10, b11), None, (b30, b31))
    opposite = ((b20_low, b21_low), (b20_high, b21_high))
    y, zl, core = at[0], at[2], at[3]
    slot = [lax.rem(zl + 4 - part, 4) for part in range(4)]
    heads = [lax.rem(y + 4 - step, 4) for step in range(4)]
    halves = [pl.multiple_of(lax.rem(core + half, 2) * 32, 32) for half in range(2)]
    kept = [{} for _ in range(TOGETHER)]

    def project_query(r):
        tokens = jnp.concatenate([x0[slot[part], r] for part in range(4)], axis=0)
        query = (dot_t(w_query_t[...], tokens) * (1.0 / math.sqrt(DEPTH))).astype(BF)
        gate = jax.nn.sigmoid(dot_t(w_gate_t[...], tokens) + gate_shift[...])
        of_head = lax.broadcasted_iota(jnp.int32, query.shape, 0) // DEPTH
        zero = jnp.zeros_like(query)
        return [jnp.where(of_head == head, query, zero) for head in heads], gate

    def project(r):
        tokens = jnp.concatenate(
            [
                rows[t][s, r, pl.ds(halves[half], 32), :]
                for half in range(2)
                for s in range(4)
                for t in range(4)
            ],
            axis=0,
        )
        key_ref[r] = dot(tokens, w_key[...]).astype(BF)
        value_ref[r] = dot_t(w_value_t[...], tokens).astype(BF)
        kept[r]["query"], kept[r]["gate"] = project_query(r)

    def score(r, a, c, query):
        half, s = divmod(c, 4)
        low = lax.rem(zl + 4 - s, 4)
        if a == 2:
            added = [opposite[zh][half][low] for zh in range(2)]
        else:
            added = [bias[a][half][zh * 4 + low] for zh in range(2)]
        added = jnp.concatenate(added, axis=1)
        return dot(key_ref[r, c * 128 : (c + 1) * 128, :], query[a]) + added

    def raise_plain(r, a):
        total = None
        for c in range(8):
            raised = jnp.exp(score(r, a, c, kept[r]["query"]))
            score_ref[r, a, c] = raised
            total = fold(jnp.add, total, jnp.sum(raised.reshape(16, 8, 256), axis=0))
        return jnp.sum(total, axis=0, keepdims=True)

    def raise_shifted(r, a, query):
        largest = None
        for c in range(8):
            scores = score(r, a, c, query)
            score_ref[r, a, c] = scores
            largest = fold(
                jnp.maximum, largest, jnp.max(scores.reshape(16, 8, 256), axis=0)
            )
        largest = jnp.max(largest, axis=0, keepdims=True)
        total = None
        for c in range(8):
            raised = jnp.exp(score_ref[r, a, c] - largest)
            score_ref[r, a, c] = raised
            total = fold(jnp.add, total, jnp.sum(raised.reshape(16, 8, 256), axis=0))
        return jnp.sum(total, axis=0, keepdims=True)

    def weigh(r, a, total):
        scale = 1.0 / total
        weights = jnp.concatenate(
            [(score_ref[r, a, c] * scale).astype(BF) for c in range(8)], axis=0
        )
        own = pl.ds(pl.multiple_of(heads[a] * DEPTH, DEPTH), DEPTH)
        attended_ref[r, own, :] = dot(value_ref[r, own, :], weights)

    def finish(r, gate):
        gated = (gate * attended_ref[r]).astype(BF)
        update = lax.dot_general(
            gated, w_out[...], (((0,), (0,)), ((), ())), preferred_element_type=F32
        )
        update = (update + out_shift[...]).astype(BF)
        for part in range(4):
            out[slot[part], r] = update[part * 64 : (part + 1) * 64]

    for r in range(TOGETHER):
        project(r)
    totals = {}
    for r in range(TOGETHER):
        for a in range(4):
            totals[r, a] = raise_plain(r, a)
    for r in range(TOGETHER):
        for a in range(4):
            weigh(r, a, totals[r, a])
    for r in range(TOGETHER):
        finish(r, kept[r]["gate"])

    safe = None
    for total in totals.values():
        inside = jnp.logical_and(total > 2.0**-60, total < 2.0**120)
        safe = fold(jnp.minimum, safe, jnp.where(inside, 1.0, 0.0))

    @pl.when(jnp.min(safe) < 0.5)
    def _():
        for r in range(TOGETHER):
            query, gate = project_query(r)
            for a in range(4):
                weigh(r, a, raise_shifted(r, a, query))
            finish(r, gate)


def attend(at, rows, biases, *weights):
    whole = lambda a: pl.BlockSpec(a.shape, lambda i, at: (0,) * a.ndim)
    block = (4, TOGETHER, 64, 128)
    if len(rows) == 4:
        count = rows[0].shape[1]
        specs = [pl.BlockSpec(block, lambda i, at: (0, i, 0, 0))] * 4
    else:
        count = rows[1].shape[2]
        specs = [pl.BlockSpec(block, lambda i, at: (0, i, 0, 0))] + [
            pl.BlockSpec(
                (None, *block),
                lambda i, at, step=step: (lax.rem(at[1] + 4 - step, 4), 0, i, 0, 0),
            )
            for step in range(1, 4)
        ]
        rows = (rows[0],) + (rows[1],) * 3
    biases = [b for pair in biases for b in pair]
    return pl.pallas_call(
        attend_kernel,
        out_shape=jax.ShapeDtypeStruct((4, count, 64, 128), BF),
        grid_spec=pltpu.PrefetchScalarGridSpec(
            num_scalar_prefetch=1,
            grid=(count // TOGETHER,),
            in_specs=specs
            + [whole(a) for a in biases]
            + [whole(a) for a in weights],
            out_specs=pl.BlockSpec(block, lambda i, at: (0, i, 0, 0)),
            scratch_shapes=[
                pltpu.VMEM((TOGETHER, 1024, 128), BF),
                pltpu.VMEM((TOGETHER, 128, 1024), BF),
                pltpu.VMEM((TOGETHER, 4, 8, 128, 256), F32),
                pltpu.VMEM((TOGETHER, 128, 256), F32),
            ],
        ),
        compiler_params=pltpu.CompilerParams(
            vmem_limit_bytes=48 << 20, dimension_semantics=("arbitrary",)
        ),
        cost_estimate=pl.CostEstimate(
            flops=count * 300_000_000,
            bytes_accessed=count << 20,
            transcendentals=count << 20,
        ),
        name="attention",
    )(at, *rows, *biases, *weights)


def normalize(values, gain, shift):
    values = values.astype(F32)
    mean = jnp.mean(values, axis=-1, keepdims=True)
    centred = values - mean
    spread = jnp.mean(centred * centred, axis=-1, keepdims=True)
    return (centred * lax.rsqrt(spread + 1e-05) * gain + shift).astype(BF)


def stack_kernel(*refs):
    *pieces, _, out = refs
    for at, piece in enumerate(pieces):
        out[at] = piece[...]


def stack_after(pieces, after):
    return pl.pallas_call(
        stack_kernel,
        out_shape=jax.ShapeDtypeStruct((len(pieces), *pieces[0].shape), BF),
        in_specs=[pl.BlockSpec(memory_space=pltpu.VMEM)] * len(pieces)
        + [pl.BlockSpec(memory_space=pl.ANY)],
        out_specs=pl.BlockSpec(memory_space=pltpu.VMEM),
        name="stack_rows",
    )(*pieces, after)


def assemble_kernel(at, *refs):
    *blocks, out = refs
    count = blocks[0].shape[0]
    for i, block in enumerate(blocks):
        chunk, step = divmod(i, 4)
        start = lax.rem(at[2] + step, 4) * 16 + chunk * count
        out[pl.ds(start, count)] = block[...]


def assemble(at, blocks):
    return pl.pallas_call(
        assemble_kernel,
        out_shape=jax.ShapeDtypeStruct((64, 64, 128), BF),
        in_specs=[pl.BlockSpec(memory_space=pltpu.SMEM)]
        + [pl.BlockSpec(memory_space=pltpu.VMEM)] * len(blocks),
        out_specs=pl.BlockSpec(memory_space=pltpu.VMEM),
        name="assemble_update",
    )(at, *blocks)


def tie_kernel(array, *rest):
    pass


def after(array, *earlier):
    return pl.pallas_call(
        tie_kernel,
        out_shape=jax.ShapeDtypeStruct(array.shape, array.dtype),
        in_specs=[pl.BlockSpec(memory_space=pl.ANY)] * (1 + len(earlier)),
        out_specs=pl.BlockSpec(memory_space=pl.ANY),
        input_output_aliases={0: 0},
        name="tie",
    )(array, *earlier)


AXES = ("y", "zh", "core", "x", "zl")


def move(array, to):
    pairs = []
    for source in range(256):
        row, col = divmod(source, 16)
        y, zh, core = row // 4, row // 2 % 2, row % 2
        x, zl = divmod(col, 4)
        y, z, core, x = to(y, zh * 4 + zl, core, x)
        y, z, x = y % 4, z % 8, x % 4
        target = ((y * 2 + z // 4) * 2 + core) * 16 + x * 4 + z % 4
        pairs.append((source, target))
    return lax.ppermute(array, AXES, pairs)


def swap_cores(array):
    return move(array, lambda y, z, core, x: (y, z, 1 - core, x))


def turn(z, step):
    return z // 4 * 4 + (z + step) % 4


def on_device(
    pair,
    norm_gain,
    norm_shift,
    w_query,
    w_key,
    w_value,
    w_gate,
    gate_shift,
    w_bias,
    w_out,
    out_shift,
):
    y, core, x, zl = (lax.axis_index(name) for name in ("y", "core", "x", "zl"))
    place = jnp.stack([y, x, zl, core]).astype(jnp.int32)
    normed = normalize(pair, norm_gain, norm_shift)
    count = 16 // CHUNKS

    def exchange(chunk):
        pieces = []
        for step in range(4):
            part = lax.dynamic_slice_in_dim(
                normed, (zl + step) % 4 * 16 + chunk * count, count, 0
            )
            if step:
                part = move(part, lambda y, z, core, x: (y, turn(z, step), core, x))
            pieces.append(part)
        return pieces

    with jax.named_scope("bias"):
        tile = jnp.einsum(
            "jkc,ch->hkj", normed.astype(F32), w_bias, precision=lax.Precision.HIGHEST
        )
        kept = lax.dynamic_slice_in_dim(tile, core * 32, 32, 1)
        sent = lax.dynamic_slice_in_dim(tile, (1 - core) * 32, 32, 1)
        got = swap_cores(sent)
        tile = jnp.where(
            core == 0, jnp.concatenate([kept, got], 2), jnp.concatenate([got, kept], 2)
        )
        rounds = []
        for step in range(4):
            part = lax.dynamic_index_in_dim(tile, (x + step) % 4, 0, keepdims=False)
            rounds.append(move(part, lambda y, z, core, x: (x + step, z, core, y)))
        rounds = jnp.stack(rounds + rounds[:3])
        block = lax.dynamic_slice_in_dim(rounds, (y - x) % 4, 4, 0).reshape(128, 128)
        along_z = lax.all_to_all(
            jnp.broadcast_to(block[None], (8, 128, 128)),
            ("zh", "zl"),
            split_axis=0,
            concat_axis=0,
            tiled=True,
        )
    with jax.named_scope("rows"):
        held = stack_after(exchange(0), block)
        rows = [(held, lax.all_gather(held, "x", axis=0, tiled=False))]
    with jax.named_scope("bias"):
        below = move(along_z, lambda y, z, core, x: (y + 1, z, core, x))
        above = move(along_z, lambda y, z, core, x: (y - 1, z, core, x))
        low = move(below[:4], lambda y, z, core, x: (y + 1, z, core, x))
        high = move(above[4:], lambda y, z, core, x: (y - 1, z, core, x))
        biases = [(b, swap_cores(b)) for b in (along_z, below, low, high, above)]
    with jax.named_scope("rows"):
        held = stack_after(exchange(1), along_z)
        left = move(held, lambda y, z, core, x: (y, z, core, x + 1))
        right = move(held, lambda y, z, core, x: (y, z, core, x - 1))
        across = jnp.concatenate(
            [
                move(left[:, :4], lambda y, z, core, x: (y, z, core, x + 1)),
                move(right[:, 4:], lambda y, z, core, x: (y, z, core, x - 1)),
            ],
            axis=1,
        )
        rows.append((held, left, across, right))
    blocks = []
    for chunk in range(CHUNKS):
        with jax.named_scope("attention"):
            part = attend(
                place,
                rows[chunk],
                biases,
                w_key,
                w_value.T,
                w_query.T,
                w_gate.T,
                gate_shift[:, None],
                w_out,
                out_shift[None],
            )
            place = after(place, part)
        with jax.named_scope("update"):
            for step in range(4):
                back = part[step]
                if step:
                    back = move(back, lambda y, z, core, x: (y, turn(z, -step), core, x))
                blocks.append(back)
    return assemble(place, blocks)


def solution(mesh):
    parts = Mesh(mesh.devices.reshape(4, 2, 2, 4, 4), AXES)
    tiles = P(("y", "zh", "core"), ("x", "zl"), None)
    return jax.shard_map(
        on_device,
        mesh=parts,
        in_specs=(tiles,) + (P(),) * 10,
        out_specs=tiles,
        check_vma=False,
    )
```

```python
import functools
import math

import jax
import jax.numpy as jnp
from jax import lax
from jax.experimental import pallas as pl
from jax.experimental.pallas import tpu as pltpu
from jax.sharding import Mesh
from jax.sharding import PartitionSpec as P

F32 = jnp.float32
BF = jnp.bfloat16
CHUNKS = 2
TOGETHER = 2
DEPTH = 32


def dot(a, b):
    return jnp.dot(a, b, preferred_element_type=F32)


def dot_t(a, b):
    return lax.dot_general(a, b, (((1,), (1,)), ((), ())), preferred_element_type=F32)


def fold(function, so_far, value):
    return value if so_far is None else function(so_far, value)


def attend_kernel(
    at,
    x0,
    x1,
    x2,
    x3,
    b00,
    b01,
    b10,
    b11,
    b20,
    b21,
    b30,
    b31,
    w_key,
    w_value_t,
    w_query_t,
    w_gate_t,
    gate_shift,
    w_out,
    out_shift,
    out,
    key_ref,
    value_ref,
    score_ref,
    attended_ref,
):
    rows = (x0, x1, x2, x3)
    bias = ((b00, b01), (b10, b11), (b20, b21), (b30, b31))
    y, zl, core = at[0], at[2], at[3]
    slot = [lax.rem(zl + 4 - part, 4) for part in range(4)]
    heads = [lax.rem(y + 4 - step, 4) for step in range(4)]
    halves = [pl.multiple_of(lax.rem(core + half, 2) * 32, 32) for half in range(2)]
    kept = [{} for _ in range(TOGETHER)]

    def project_query(r):
        tokens = jnp.concatenate([x0[slot[part], r] for part in range(4)], axis=0)
        query = (dot_t(w_query_t[...], tokens) * (1.0 / math.sqrt(DEPTH))).astype(BF)
        gate = jax.nn.sigmoid(dot_t(w_gate_t[...], tokens) + gate_shift[...])
        of_head = lax.broadcasted_iota(jnp.int32, query.shape, 0) // DEPTH
        zero = jnp.zeros_like(query)
        return [jnp.where(of_head == head, query, zero) for head in heads], gate

    def project(r):
        tokens = jnp.concatenate(
            [
                rows[t][s, r, pl.ds(halves[half], 32), :]
                for half in range(2)
                for s in range(4)
                for t in range(4)
            ],
            axis=0,
        )
        key_ref[r] = dot(tokens, w_key[...]).astype(BF)
        value_ref[r] = dot_t(w_value_t[...], tokens).astype(BF)
        kept[r]["query"], kept[r]["gate"] = project_query(r)

    def score(r, a, c, query):
        half, s = divmod(c, 4)
        z_of = [zh * 4 + lax.rem(zl + 4 - s, 4) for zh in range(2)]
        added = jnp.concatenate([bias[a][half][z] for z in z_of], axis=1)
        return dot(key_ref[r, c * 128 : (c + 1) * 128, :], query[a]) + added

    def raise_plain(r, a):
        total = None
        for c in range(8):
            raised = jnp.exp(score(r, a, c, kept[r]["query"]))
            score_ref[r, a, c] = raised
            total = fold(jnp.add, total, jnp.sum(raised.reshape(16, 8, 256), axis=0))
        return jnp.sum(total, axis=0, keepdims=True)

    def raise_shifted(r, a, query):
        largest = None
        for c in range(8):
            scores = score(r, a, c, query)
            score_ref[r, a, c] = scores
            largest = fold(
                jnp.maximum, largest, jnp.max(scores.reshape(16, 8, 256), axis=0)
            )
        largest = jnp.max(largest, axis=0, keepdims=True)
        total = None
        for c in range(8):
            raised = jnp.exp(score_ref[r, a, c] - largest)
            score_ref[r, a, c] = raised
            total = fold(jnp.add, total, jnp.sum(raised.reshape(16, 8, 256), axis=0))
        return jnp.sum(total, axis=0, keepdims=True)

    def weigh(r, a, total):
        scale = 1.0 / total
        weights = jnp.concatenate(
            [(score_ref[r, a, c] * scale).astype(BF) for c in range(8)], axis=0
        )
        own = pl.ds(pl.multiple_of(heads[a] * DEPTH, DEPTH), DEPTH)
        attended_ref[r, own, :] = dot(value_ref[r, own, :], weights)

    def finish(r, gate):
        gated = (gate * attended_ref[r]).astype(BF)
        update = lax.dot_general(
            gated, w_out[...], (((0,), (0,)), ((), ())), preferred_element_type=F32
        )
        update = (update + out_shift[...]).astype(BF)
        for part in range(4):
            out[slot[part], r] = update[part * 64 : (part + 1) * 64]

    for r in range(TOGETHER):
        project(r)
    totals = {}
    for r in range(TOGETHER):
        for a in range(4):
            totals[r, a] = raise_plain(r, a)
    for r in range(TOGETHER):
        for a in range(4):
            weigh(r, a, totals[r, a])
    for r in range(TOGETHER):
        finish(r, kept[r]["gate"])

    safe = None
    for total in totals.values():
        inside = jnp.logical_and(total > 2.0**-60, total < 2.0**120)
        safe = fold(jnp.minimum, safe, jnp.where(inside, 1.0, 0.0))

    @pl.when(jnp.min(safe) < 0.5)
    def _():
        for r in range(TOGETHER):
            query, gate = project_query(r)
            for a in range(4):
                weigh(r, a, raise_shifted(r, a, query))
            finish(r, gate)


def attend(at, rows, first, biases, *weights):
    count = 16 // CHUNKS
    whole = lambda a: pl.BlockSpec(a.shape, lambda i, at: (0,) * a.ndim)
    block = (4, TOGETHER, 64, 128)
    specs = [
        pl.BlockSpec(block, lambda i, at, start=start // TOGETHER: (0, i + start, 0, 0))
        for start in first
    ]
    biases = [b for pair in biases for b in pair]
    return pl.pallas_call(
        attend_kernel,
        out_shape=jax.ShapeDtypeStruct((4, count, 64, 128), BF),
        grid_spec=pltpu.PrefetchScalarGridSpec(
            num_scalar_prefetch=1,
            grid=(count // TOGETHER,),
            in_specs=specs
            + [whole(a) for a in biases]
            + [whole(a) for a in weights],
            out_specs=pl.BlockSpec(block, lambda i, at: (0, i, 0, 0)),
            scratch_shapes=[
                pltpu.VMEM((TOGETHER, 1024, 128), BF),
                pltpu.VMEM((TOGETHER, 128, 1024), BF),
                pltpu.VMEM((TOGETHER, 4, 8, 128, 256), F32),
                pltpu.VMEM((TOGETHER, 128, 256), F32),
            ],
        ),
        compiler_params=pltpu.CompilerParams(
            vmem_limit_bytes=48 << 20, dimension_semantics=("arbitrary",)
        ),
        cost_estimate=pl.CostEstimate(
            flops=count * 300_000_000,
            bytes_accessed=count << 20,
            transcendentals=count << 20,
        ),
        name="attention",
    )(at, *rows, *biases, *weights)


def normalize(values, gain, shift):
    values = values.astype(F32)
    mean = jnp.mean(values, axis=-1, keepdims=True)
    centred = values - mean
    spread = jnp.mean(centred * centred, axis=-1, keepdims=True)
    return (centred * lax.rsqrt(spread + 1e-05) * gain + shift).astype(BF)


def assemble_kernel(at, *refs):
    *blocks, out = refs
    count = blocks[0].shape[0]
    for i, block in enumerate(blocks):
        chunk, step = divmod(i, 4)
        start = lax.rem(at[2] + step, 4) * 16 + chunk * count
        out[pl.ds(start, count)] = block[...]


def assemble(at, blocks):
    return pl.pallas_call(
        assemble_kernel,
        out_shape=jax.ShapeDtypeStruct((64, 64, 128), BF),
        in_specs=[pl.BlockSpec(memory_space=pltpu.SMEM)]
        + [pl.BlockSpec(memory_space=pltpu.VMEM)] * len(blocks),
        out_specs=pl.BlockSpec(memory_space=pltpu.VMEM),
        name="assemble_update",
    )(at, *blocks)


def tie_kernel(array, *rest):
    pass


def after(array, *earlier):
    return pl.pallas_call(
        tie_kernel,
        out_shape=jax.ShapeDtypeStruct(array.shape, array.dtype),
        in_specs=[pl.BlockSpec(memory_space=pl.ANY)] * (1 + len(earlier)),
        out_specs=pl.BlockSpec(memory_space=pl.ANY),
        input_output_aliases={0: 0},
        name="tie",
    )(array, *earlier)


AXES = ("y", "zh", "core", "x", "zl")


def move(array, to):
    pairs = []
    for source in range(256):
        row, col = divmod(source, 16)
        y, zh, core = row // 4, row // 2 % 2, row % 2
        x, zl = divmod(col, 4)
        y, z, core, x = to(y, zh * 4 + zl, core, x)
        y, z, x = y % 4, z % 8, x % 4
        target = ((y * 2 + z // 4) * 2 + core) * 16 + x * 4 + z % 4
        pairs.append((source, target))
    return lax.ppermute(array, AXES, pairs)


def swap_cores(array):
    return move(array, lambda y, z, core, x: (y, z, 1 - core, x))


def turn(z, step):
    return z // 4 * 4 + (z + step) % 4


def on_device(
    pair,
    norm_gain,
    norm_shift,
    w_query,
    w_key,
    w_value,
    w_gate,
    gate_shift,
    w_bias,
    w_out,
    out_shift,
):
    y, core, x, zl = (lax.axis_index(name) for name in ("y", "core", "x", "zl"))
    place = jnp.stack([y, x, zl, core]).astype(jnp.int32)
    normed = normalize(pair, norm_gain, norm_shift)
    count = 16 // CHUNKS

    with jax.named_scope("rows"):
        pieces = []
        for step in range(4):
            part = lax.dynamic_slice_in_dim(normed, (zl + step) % 4 * 16, 16, 0)
            if step:
                part = move(part, lambda y, z, core, x: (y, turn(z, step), core, x))
            pieces.append(part)
        here = jnp.stack(pieces)
        left = move(here, lambda y, z, core, x: (y, z, core, x + 1))
        right = move(here, lambda y, z, core, x: (y, z, core, x - 1))
        across = (
            move(left[:, :count], lambda y, z, core, x: (y, z, core, x + 1)),
            move(right[:, count:], lambda y, z, core, x: (y, z, core, x - 1)),
        )
    with jax.named_scope("bias"):
        tile = jnp.einsum(
            "jkc,ch->hkj", normed.astype(F32), w_bias, precision=lax.Precision.HIGHEST
        )
        kept = lax.dynamic_slice_in_dim(tile, core * 32, 32, 1)
        sent = lax.dynamic_slice_in_dim(tile, (1 - core) * 32, 32, 1)
        got = swap_cores(sent)
        tile = jnp.where(
            core == 0, jnp.concatenate([kept, got], 2), jnp.concatenate([got, kept], 2)
        )
        rounds = []
        for step in range(4):
            part = lax.dynamic_index_in_dim(tile, (x + step) % 4, 0, keepdims=False)
            rounds.append(move(part, lambda y, z, core, x: (x + step, z, core, y)))
        rounds = jnp.stack(rounds + rounds[:3])
        block = lax.dynamic_slice_in_dim(rounds, (y - x) % 4, 4, 0).reshape(128, 128)
        block = after(block, here)
        along_z = lax.all_to_all(
            jnp.broadcast_to(block[None], (8, 128, 128)),
            ("zh", "zl"),
            split_axis=0,
            concat_axis=0,
            tiled=True,
        )
    with jax.named_scope("bias"):
        along_z = after(along_z, left, right)
        biases = []
        for step in range(4):
            moved = along_z
            if step:
                moved = move(along_z, lambda y, z, core, x: (y + step, z, core, x))
            biases.append((moved, swap_cores(moved)))
    blocks = []
    for chunk in range(CHUNKS):
        with jax.named_scope("attention"):
            part = attend(
                place,
                (here, left, across[chunk], right),
                (chunk * count, chunk * count, 0, chunk * count),
                biases,
                w_key,
                w_value.T,
                w_query.T,
                w_gate.T,
                gate_shift[:, None],
                w_out,
                out_shift[None],
            )
            place = after(place, part)
        with jax.named_scope("update"):
            for step in range(4):
                back = part[step]
                if step:
                    back = move(back, lambda y, z, core, x: (y, turn(z, -step), core, x))
                blocks.append(back)
    return assemble(place, blocks)


def solution(mesh):
    parts = Mesh(mesh.devices.reshape(4, 2, 2, 4, 4), AXES)
    tiles = P(("y", "zh", "core"), ("x", "zl"), None)
    return jax.shard_map(
        on_device,
        mesh=parts,
        in_specs=(tiles,) + (P(),) * 10,
        out_specs=tiles,
        check_vma=False,
    )
```

```python
import functools
import math

import jax
import jax.numpy as jnp
from jax import lax
from jax.experimental import pallas as pl
from jax.experimental.pallas import tpu as pltpu
from jax.sharding import Mesh
from jax.sharding import PartitionSpec as P

F32 = jnp.float32
BF = jnp.bfloat16
CHUNKS = 2
TOGETHER = 2
DEPTH = 32


def dot(a, b):
    return jnp.dot(a, b, preferred_element_type=F32)


def dot_t(a, b):
    return lax.dot_general(a, b, (((1,), (1,)), ((), ())), preferred_element_type=F32)


def fold(function, so_far, value):
    return value if so_far is None else function(so_far, value)


def attend_kernel(
    at,
    x0,
    x1,
    x2,
    x3,
    b00,
    b01,
    b10,
    b11,
    b20,
    b21,
    b30,
    b31,
    w_key,
    w_value_t,
    w_query_t,
    w_gate_t,
    gate_shift,
    w_out,
    out_shift,
    out0,
    out1,
    out2,
    out3,
    key_ref,
    value_ref,
    score_ref,
    attended_ref,
    update_ref,
):
    rows = (x0, x1, x2, x3)
    bias = ((b00, b01), (b10, b11), (b20, b21), (b30, b31))
    y, zl, core = at[0], at[2], at[3]
    slot = [lax.rem(zl + 4 - part, 4) for part in range(4)]
    heads = [lax.rem(y + 4 - step, 4) for step in range(4)]
    halves = [pl.multiple_of(lax.rem(core + half, 2) * 32, 32) for half in range(2)]
    kept = [{} for _ in range(TOGETHER)]

    def project_query(r):
        tokens = jnp.concatenate([x0[r, slot[part]] for part in range(4)], axis=0)
        query = (dot_t(w_query_t[...], tokens) * (1.0 / math.sqrt(DEPTH))).astype(BF)
        gate = jax.nn.sigmoid(dot_t(w_gate_t[...], tokens) + gate_shift[...])
        of_head = lax.broadcasted_iota(jnp.int32, query.shape, 0) // DEPTH
        zero = jnp.zeros_like(query)
        return [jnp.where(of_head == head, query, zero) for head in heads], gate

    def project(r):
        tokens = jnp.concatenate(
            [
                rows[t][r, s, pl.ds(halves[half], 32), :]
                for half in range(2)
                for s in range(4)
                for t in range(4)
            ],
            axis=0,
        )
        key_ref[r] = dot(tokens, w_key[...]).astype(BF)
        value_ref[r] = dot_t(w_value_t[...], tokens).astype(BF)
        kept[r]["query"], kept[r]["gate"] = project_query(r)

    def score(r, a, c, query):
        half, s = divmod(c, 4)
        z_of = [zh * 4 + lax.rem(zl + 4 - s, 4) for zh in range(2)]
        added = jnp.concatenate([bias[a][half][z] for z in z_of], axis=1)
        return dot(key_ref[r, c * 128 : (c + 1) * 128, :], query[a]) + added

    def raise_plain(r, a):
        total = None
        for c in range(8):
            raised = jnp.exp(score(r, a, c, kept[r]["query"]))
            score_ref[r, a, c] = raised
            total = fold(jnp.add, total, jnp.sum(raised.reshape(16, 8, 256), axis=0))
        return jnp.sum(total, axis=0, keepdims=True)

    def raise_shifted(r, a, query):
        largest = None
        for c in range(8):
            scores = score(r, a, c, query)
            score_ref[r, a, c] = scores
            largest = fold(
                jnp.maximum, largest, jnp.max(scores.reshape(16, 8, 256), axis=0)
            )
        largest = jnp.max(largest, axis=0, keepdims=True)
        total = None
        for c in range(8):
            raised = jnp.exp(score_ref[r, a, c] - largest)
            score_ref[r, a, c] = raised
            total = fold(jnp.add, total, jnp.sum(raised.reshape(16, 8, 256), axis=0))
        return jnp.sum(total, axis=0, keepdims=True)

    def weigh(r, a, total):
        scale = 1.0 / total
        weights = jnp.concatenate(
            [(score_ref[r, a, c] * scale).astype(BF) for c in range(8)], axis=0
        )
        own = pl.ds(pl.multiple_of(heads[a] * DEPTH, DEPTH), DEPTH)
        attended_ref[r, own, :] = dot(value_ref[r, own, :], weights)

    def finish(r, gate):
        gated = (gate * attended_ref[r]).astype(BF)
        update = lax.dot_general(
            gated, w_out[...], (((0,), (0,)), ((), ())), preferred_element_type=F32
        )
        update_ref[r] = (update + out_shift[...]).astype(BF)
        for s, out in enumerate((out0, out1, out2, out3)):
            start = pl.multiple_of(slot[s] * 64, 64)
            out[r] = update_ref[r, pl.ds(start, 64), :]

    for r in range(TOGETHER):
        project(r)
    totals = {}
    for r in range(TOGETHER):
        for a in range(4):
            totals[r, a] = raise_plain(r, a)
    for r in range(TOGETHER):
        for a in range(4):
            weigh(r, a, totals[r, a])
    for r in range(TOGETHER):
        finish(r, kept[r]["gate"])

    safe = None
    for total in totals.values():
        inside = jnp.logical_and(total > 2.0**-60, total < 2.0**120)
        safe = fold(jnp.minimum, safe, jnp.where(inside, 1.0, 0.0))

    @pl.when(jnp.min(safe) < 0.5)
    def _():
        for r in range(TOGETHER):
            query, gate = project_query(r)
            for a in range(4):
                weigh(r, a, raise_shifted(r, a, query))
            finish(r, gate)


def attend(at, rows, first, biases, *weights):
    count = 16 // CHUNKS
    whole = lambda a: pl.BlockSpec(a.shape, lambda i, at: (0,) * a.ndim)
    block = (TOGETHER, 4, 64, 128)
    specs = [
        pl.BlockSpec(block, lambda i, at, start=start // TOGETHER: (i + start, 0, 0, 0))
        for start in first
    ]
    biases = [b for pair in biases for b in pair]
    return pl.pallas_call(
        attend_kernel,
        out_shape=[jax.ShapeDtypeStruct((count, 64, 128), BF)] * 4,
        grid_spec=pltpu.PrefetchScalarGridSpec(
            num_scalar_prefetch=1,
            grid=(count // TOGETHER,),
            in_specs=specs
            + [whole(a) for a in biases]
            + [whole(a) for a in weights],
            out_specs=[pl.BlockSpec((TOGETHER, 64, 128), lambda i, at: (i, 0, 0))] * 4,
            scratch_shapes=[
                pltpu.VMEM((TOGETHER, 1024, 128), BF),
                pltpu.VMEM((TOGETHER, 128, 1024), BF),
                pltpu.VMEM((TOGETHER, 4, 8, 128, 256), F32),
                pltpu.VMEM((TOGETHER, 128, 256), F32),
                pltpu.VMEM((TOGETHER, 256, 128), BF),
            ],
        ),
        compiler_params=pltpu.CompilerParams(
            vmem_limit_bytes=48 << 20, dimension_semantics=("arbitrary",)
        ),
        cost_estimate=pl.CostEstimate(
            flops=count * 300_000_000,
            bytes_accessed=count << 20,
            transcendentals=count << 20,
        ),
        name="attention",
    )(at, *rows, *biases, *weights)


def normalize_kernel(at, pair, gain, shift, normed, cut0, cut1, cut2, cut3):
    for step, cut in enumerate((cut0, cut1, cut2, cut3)):
        start = lax.rem(at[2] + step, 4) * 16
        for i in range(0, 16, 4):
            values = pair[pl.ds(start + i, 4)].astype(F32)
            mean = jnp.mean(values, axis=-1, keepdims=True)
            centred = values - mean
            spread = jnp.mean(centred * centred, axis=-1, keepdims=True)
            scaled = centred * lax.rsqrt(spread + 1e-05) * gain[...] + shift[...]
            scaled = scaled.astype(BF)
            normed[pl.ds(start + i, 4)] = scaled
            cut[i : i + 4] = scaled


def normalize(at, pair, gain, shift):
    vmem = pl.BlockSpec(memory_space=pltpu.VMEM)
    cut = jax.ShapeDtypeStruct((16, 64, 128), BF)
    normed, *cuts = pl.pallas_call(
        normalize_kernel,
        out_shape=[jax.ShapeDtypeStruct(pair.shape, BF)] + [cut] * 4,
        in_specs=[pl.BlockSpec(memory_space=pltpu.SMEM), vmem, vmem, vmem],
        out_specs=[vmem] * 5,
        name="normalize",
    )(at, pair, gain[None, None], shift[None, None])
    return normed, cuts


def assemble_kernel(at, *refs):
    *blocks, out, done = refs
    count = blocks[0].shape[0]
    copies = []
    for i, block in enumerate(blocks):
        chunk, step = divmod(i, 4)
        start = lax.rem(at[2] + step, 4) * 16 + chunk * count
        copies.append(
            pltpu.make_async_copy(block, out.at[pl.ds(start, count)], done.at[i])
        )
    for copy in copies:
        copy.start()
    for copy in copies:
        copy.wait()


def assemble(at, blocks):
    return pl.pallas_call(
        assemble_kernel,
        out_shape=jax.ShapeDtypeStruct((64, 64, 128), BF),
        in_specs=[pl.BlockSpec(memory_space=pltpu.SMEM)]
        + [pl.BlockSpec(memory_space=pl.ANY)] * len(blocks),
        out_specs=pl.BlockSpec(memory_space=pl.ANY),
        scratch_shapes=[pltpu.SemaphoreType.DMA((len(blocks),))],
        name="assemble_update",
    )(at, *blocks)


def tie_kernel(array, *rest):
    pass


def after(array, *earlier):
    return pl.pallas_call(
        tie_kernel,
        out_shape=jax.ShapeDtypeStruct(array.shape, array.dtype),
        in_specs=[pl.BlockSpec(memory_space=pl.ANY)] * (1 + len(earlier)),
        out_specs=pl.BlockSpec(memory_space=pl.ANY),
        input_output_aliases={0: 0},
        name="tie",
    )(array, *earlier)


AXES = ("y", "zh", "core", "x", "zl")


def move(array, to):
    pairs = []
    for source in range(256):
        row, col = divmod(source, 16)
        y, zh, core = row // 4, row // 2 % 2, row % 2
        x, zl = divmod(col, 4)
        y, z, core, x = to(y, zh * 4 + zl, core, x)
        y, z, x = y % 4, z % 8, x % 4
        target = ((y * 2 + z // 4) * 2 + core) * 16 + x * 4 + z % 4
        pairs.append((source, target))
    return lax.ppermute(array, AXES, pairs)


def swap_cores(array):
    return move(array, lambda y, z, core, x: (y, z, 1 - core, x))


def turn(z, step):
    return z // 4 * 4 + (z + step) % 4


def on_device(
    pair,
    norm_gain,
    norm_shift,
    w_query,
    w_key,
    w_value,
    w_gate,
    gate_shift,
    w_bias,
    w_out,
    out_shift,
):
    y, core, x, zl = (lax.axis_index(name) for name in ("y", "core", "x", "zl"))
    place = jnp.stack([y, x, zl, core]).astype(jnp.int32)
    normed, cuts = normalize(place, pair, norm_gain, norm_shift)
    count = 16 // CHUNKS

    with jax.named_scope("rows"):
        pieces = []
        for step in range(4):
            part = cuts[step]
            if step:
                part = move(part, lambda y, z, core, x: (y, turn(z, step), core, x))
            pieces.append(part)
        here = jnp.stack(pieces, axis=1)
        left = move(here, lambda y, z, core, x: (y, z, core, x + 1))
        right = move(here, lambda y, z, core, x: (y, z, core, x - 1))
        across = (
            move(left[:count], lambda y, z, core, x: (y, z, core, x + 1)),
            move(right[count:], lambda y, z, core, x: (y, z, core, x - 1)),
        )
    with jax.named_scope("bias"):
        tile = jnp.einsum(
            "jkc,ch->hkj", normed.astype(F32), w_bias, precision=lax.Precision.HIGHEST
        )
        kept = lax.dynamic_slice_in_dim(tile, core * 32, 32, 1)
        sent = lax.dynamic_slice_in_dim(tile, (1 - core) * 32, 32, 1)
        got = swap_cores(sent)
        tile = jnp.where(
            core == 0, jnp.concatenate([kept, got], 2), jnp.concatenate([got, kept], 2)
        )
        rounds = []
        for step in range(4):
            part = lax.dynamic_index_in_dim(tile, (x + step) % 4, 0, keepdims=False)
            rounds.append(move(part, lambda y, z, core, x: (x + step, z, core, y)))
        rounds = jnp.stack(rounds + rounds[:3])
        block = lax.dynamic_slice_in_dim(rounds, (y - x) % 4, 4, 0).reshape(128, 128)
        block = after(block, *[piece[0] for piece in pieces[1:]])
        along_z = lax.all_to_all(
            jnp.broadcast_to(block[None], (8, 128, 128)),
            ("zh", "zl"),
            split_axis=0,
            concat_axis=0,
            tiled=True,
        )
    with jax.named_scope("bias"):
        along_z = after(along_z, left[0, 0], right[0, 0])
        biases = []
        for step in range(4):
            moved = along_z
            if step:
                moved = move(along_z, lambda y, z, core, x: (y + step, z, core, x))
            biases.append((moved, swap_cores(moved)))
    blocks = []
    start = place
    for chunk in range(CHUNKS):
        with jax.named_scope("attention"):
            part = attend(
                place,
                (here, left, across[chunk], right),
                (chunk * count, chunk * count, 0, chunk * count),
                biases,
                w_key,
                w_value.T,
                w_query.T,
                w_gate.T,
                gate_shift[:, None],
                w_out,
                out_shift[None],
            )
            place = after(place, part[0][0])
        with jax.named_scope("update"):
            for step in range(4):
                back = part[step]
                if step:
                    back = move(back, lambda y, z, core, x: (y, turn(z, -step), core, x))
                blocks.append(back)
    return assemble(start, blocks)


def solution(mesh):
    parts = Mesh(mesh.devices.reshape(4, 2, 2, 4, 4), AXES)
    tiles = P(("y", "zh", "core"), ("x", "zl"), None)
    return jax.shard_map(
        on_device,
        mesh=parts,
        in_specs=(tiles,) + (P(),) * 10,
        out_specs=tiles,
        check_vma=False,
    )
```

```python
import functools
import math

import jax
import jax.numpy as jnp
from jax import lax
from jax.experimental import pallas as pl
from jax.experimental.pallas import tpu as pltpu
from jax.sharding import Mesh
from jax.sharding import PartitionSpec as P

F32 = jnp.float32
BF = jnp.bfloat16
CHUNKS = 2
TOGETHER = 2
DEPTH = 32


def dot(a, b):
    return jnp.dot(a, b, preferred_element_type=F32)


def dot_t(a, b):
    return lax.dot_general(a, b, (((1,), (1,)), ((), ())), preferred_element_type=F32)


def fold(function, so_far, value):
    return value if so_far is None else function(so_far, value)


def attend_kernel(
    at,
    x0,
    x1,
    x2,
    x3,
    b00,
    b01,
    b10,
    b11,
    b20,
    b21,
    b30,
    b31,
    w_key,
    w_value_t,
    w_query_t,
    w_gate_t,
    gate_shift,
    w_out,
    out_shift,
    out,
    key_ref,
    value_ref,
    score_ref,
    attended_ref,
):
    rows = (x0, x1, x2, x3)
    bias = ((b00, b01), (b10, b11), (b20, b21), (b30, b31))
    y, zl, core = at[0], at[2], at[3]
    slot = [lax.rem(zl + 4 - part, 4) for part in range(4)]
    heads = [lax.rem(y + 4 - step, 4) for step in range(4)]
    halves = [pl.multiple_of(lax.rem(core + half, 2) * 32, 32) for half in range(2)]
    kept = [{} for _ in range(TOGETHER)]

    def project_query(r):
        tokens = jnp.concatenate([x0[slot[part], r] for part in range(4)], axis=0)
        query = (dot_t(w_query_t[...], tokens) * (1.0 / math.sqrt(DEPTH))).astype(BF)
        gate = jax.nn.sigmoid(dot_t(w_gate_t[...], tokens) + gate_shift[...])
        of_head = lax.broadcasted_iota(jnp.int32, query.shape, 0) // DEPTH
        zero = jnp.zeros_like(query)
        return [jnp.where(of_head == head, query, zero) for head in heads], gate

    def project(r):
        tokens = jnp.concatenate(
            [
                rows[t][s, r, pl.ds(halves[half], 32), :]
                for half in range(2)
                for s in range(4)
                for t in range(4)
            ],
            axis=0,
        )
        key_ref[r] = dot(tokens, w_key[...]).astype(BF)
        value_ref[r] = dot_t(w_value_t[...], tokens).astype(BF)
        kept[r]["query"], kept[r]["gate"] = project_query(r)

    def score(r, a, c, query):
        half, s = divmod(c, 4)
        z_of = [zh * 4 + lax.rem(zl + 4 - s, 4) for zh in range(2)]
        added = jnp.concatenate([bias[a][half][z] for z in z_of], axis=1)
        return dot(key_ref[r, c * 128 : (c + 1) * 128, :], query[a]) + added

    def raise_plain(r, a):
        total = None
        for c in range(8):
            raised = jnp.exp(score(r, a, c, kept[r]["query"]))
            score_ref[r, a, c] = raised
            total = fold(jnp.add, total, jnp.sum(raised.reshape(16, 8, 256), axis=0))
        return jnp.sum(total, axis=0, keepdims=True)

    def raise_shifted(r, a, query):
        largest = None
        for c in range(8):
            scores = score(r, a, c, query)
            score_ref[r, a, c] = scores
            largest = fold(
                jnp.maximum, largest, jnp.max(scores.reshape(16, 8, 256), axis=0)
            )
        largest = jnp.max(largest, axis=0, keepdims=True)
        total = None
        for c in range(8):
            raised = jnp.exp(score_ref[r, a, c] - largest)
            score_ref[r, a, c] = raised
            total = fold(jnp.add, total, jnp.sum(raised.reshape(16, 8, 256), axis=0))
        return jnp.sum(total, axis=0, keepdims=True)

    def weigh(r, a, total):
        scale = 1.0 / total
        weights = jnp.concatenate(
            [(score_ref[r, a, c] * scale).astype(BF) for c in range(8)], axis=0
        )
        own = pl.ds(pl.multiple_of(heads[a] * DEPTH, DEPTH), DEPTH)
        attended_ref[r, own, :] = dot(value_ref[r, own, :], weights)

    def finish(r, gate):
        gated = (gate * attended_ref[r]).astype(BF)
        update = lax.dot_general(
            gated, w_out[...], (((0,), (0,)), ((), ())), preferred_element_type=F32
        )
        update = (update + out_shift[...]).astype(BF)
        for part in range(4):
            out[slot[part], r] = update[part * 64 : (part + 1) * 64]

    for r in range(TOGETHER):
        project(r)
    totals = {}
    for r in range(TOGETHER):
        for a in range(4):
            totals[r, a] = raise_plain(r, a)
    for r in range(TOGETHER):
        for a in range(4):
            weigh(r, a, totals[r, a])
    for r in range(TOGETHER):
        finish(r, kept[r]["gate"])

    safe = None
    for total in totals.values():
        inside = jnp.logical_and(total > 2.0**-60, total < 2.0**120)
        safe = fold(jnp.minimum, safe, jnp.where(inside, 1.0, 0.0))

    @pl.when(jnp.min(safe) < 0.5)
    def _():
        for r in range(TOGETHER):
            query, gate = project_query(r)
            for a in range(4):
                weigh(r, a, raise_shifted(r, a, query))
            finish(r, gate)


def attend(at, rows, first, biases, *weights):
    count = 16 // CHUNKS
    whole = lambda a: pl.BlockSpec(a.shape, lambda i, at: (0,) * a.ndim)
    block = (4, TOGETHER, 64, 128)
    start = first // TOGETHER
    specs = [pl.BlockSpec(block, lambda i, at: (0, i + start, 0, 0))] * 4
    biases = [b for pair in biases for b in pair]
    return pl.pallas_call(
        attend_kernel,
        out_shape=jax.ShapeDtypeStruct((4, count, 64, 128), BF),
        grid_spec=pltpu.PrefetchScalarGridSpec(
            num_scalar_prefetch=1,
            grid=(count // TOGETHER,),
            in_specs=specs
            + [whole(a) for a in biases]
            + [whole(a) for a in weights],
            out_specs=pl.BlockSpec(block, lambda i, at: (0, i, 0, 0)),
            scratch_shapes=[
                pltpu.VMEM((TOGETHER, 1024, 128), BF),
                pltpu.VMEM((TOGETHER, 128, 1024), BF),
                pltpu.VMEM((TOGETHER, 4, 8, 128, 256), F32),
                pltpu.VMEM((TOGETHER, 128, 256), F32),
            ],
        ),
        compiler_params=pltpu.CompilerParams(
            vmem_limit_bytes=48 << 20, dimension_semantics=("arbitrary",)
        ),
        cost_estimate=pl.CostEstimate(
            flops=count * 300_000_000,
            bytes_accessed=count << 20,
            transcendentals=count << 20,
        ),
        name="attention",
    )(at, *rows, *biases, *weights)


def normalize(values, gain, shift):
    values = values.astype(F32)
    mean = jnp.mean(values, axis=-1, keepdims=True)
    centred = values - mean
    spread = jnp.mean(centred * centred, axis=-1, keepdims=True)
    return (centred * lax.rsqrt(spread + 1e-05) * gain + shift).astype(BF)


def assemble_kernel(at, *refs):
    *blocks, out = refs
    count = blocks[0].shape[0]
    for i, block in enumerate(blocks):
        chunk, step = divmod(i, 4)
        start = lax.rem(at[2] + step, 4) * 16 + chunk * count
        out[pl.ds(start, count)] = block[...]


def assemble(at, blocks):
    return pl.pallas_call(
        assemble_kernel,
        out_shape=jax.ShapeDtypeStruct((64, 64, 128), BF),
        in_specs=[pl.BlockSpec(memory_space=pltpu.SMEM)]
        + [pl.BlockSpec(memory_space=pltpu.VMEM)] * len(blocks),
        out_specs=pl.BlockSpec(memory_space=pltpu.VMEM),
        name="assemble_update",
    )(at, *blocks)


def tie_kernel(array, *rest):
    pass


def after(array, *earlier):
    return pl.pallas_call(
        tie_kernel,
        out_shape=jax.ShapeDtypeStruct(array.shape, array.dtype),
        in_specs=[pl.BlockSpec(memory_space=pl.ANY)] * (1 + len(earlier)),
        out_specs=pl.BlockSpec(memory_space=pl.ANY),
        input_output_aliases={0: 0},
        name="tie",
    )(array, *earlier)


AXES = ("y", "zh", "core", "x", "zl")


def move(array, to):
    pairs = []
    for source in range(256):
        row, col = divmod(source, 16)
        y, zh, core = row // 4, row // 2 % 2, row % 2
        x, zl = divmod(col, 4)
        y, z, core, x = to(y, zh * 4 + zl, core, x)
        y, z, x = y % 4, z % 8, x % 4
        target = ((y * 2 + z // 4) * 2 + core) * 16 + x * 4 + z % 4
        pairs.append((source, target))
    return lax.ppermute(array, AXES, pairs)


def swap_cores(array):
    return move(array, lambda y, z, core, x: (y, z, 1 - core, x))


def turn(z, step):
    return z // 4 * 4 + (z + step) % 4


def on_device(
    pair,
    norm_gain,
    norm_shift,
    w_query,
    w_key,
    w_value,
    w_gate,
    gate_shift,
    w_bias,
    w_out,
    out_shift,
):
    y, core, x, zl = (lax.axis_index(name) for name in ("y", "core", "x", "zl"))
    place = jnp.stack([y, x, zl, core]).astype(jnp.int32)
    normed = normalize(pair, norm_gain, norm_shift)
    count = 16 // CHUNKS

    with jax.named_scope("rows"):
        pieces = []
        for step in range(4):
            part = lax.dynamic_slice_in_dim(normed, (zl + step) % 4 * 16, 16, 0)
            if step:
                part = move(part, lambda y, z, core, x: (y, turn(z, step), core, x))
            pieces.append(part)
        here = jnp.stack(pieces)
        left = move(here, lambda y, z, core, x: (y, z, core, x + 1))
        right = move(here, lambda y, z, core, x: (y, z, core, x - 1))
        across = move(here, lambda y, z, core, x: (y, z, core, x + 2))
    with jax.named_scope("bias"):
        tile = jnp.einsum(
            "jkc,ch->hkj", normed.astype(F32), w_bias, precision=lax.Precision.HIGHEST
        )
        kept = lax.dynamic_slice_in_dim(tile, core * 32, 32, 1)
        sent = lax.dynamic_slice_in_dim(tile, (1 - core) * 32, 32, 1)
        got = swap_cores(sent)
        tile = jnp.where(
            core == 0, jnp.concatenate([kept, got], 2), jnp.concatenate([got, kept], 2)
        )
        rounds = []
        for step in range(4):
            part = lax.dynamic_index_in_dim(tile, (x + step) % 4, 0, keepdims=False)
            rounds.append(move(part, lambda y, z, core, x: (x + step, z, core, y)))
        rounds = jnp.stack(rounds + rounds[:3])
        block = lax.dynamic_slice_in_dim(rounds, (y - x) % 4, 4, 0).reshape(128, 128)
        block = after(block, here)
        along_z = lax.all_to_all(
            jnp.broadcast_to(block[None], (8, 128, 128)),
            ("zh", "zl"),
            split_axis=0,
            concat_axis=0,
            tiled=True,
        )
    with jax.named_scope("bias"):
        along_z = after(along_z, left, right)
        biases = []
        for step in range(4):
            moved = along_z
            if step:
                moved = move(along_z, lambda y, z, core, x: (y + step, z, core, x))
            biases.append((moved, swap_cores(moved)))
    blocks = []
    for chunk in range(CHUNKS):
        with jax.named_scope("attention"):
            part = attend(
                place,
                (here, left, across, right),
                chunk * count,
                biases,
                w_key,
                w_value.T,
                w_query.T,
                w_gate.T,
                gate_shift[:, None],
                w_out,
                out_shift[None],
            )
            place = after(place, part)
        with jax.named_scope("update"):
            for step in range(4):
                back = part[step]
                if step:
                    back = move(back, lambda y, z, core, x: (y, turn(z, -step), core, x))
                blocks.append(back)
    return assemble(place, blocks)


def solution(mesh):
    parts = Mesh(mesh.devices.reshape(4, 2, 2, 4, 4), AXES)
    tiles = P(("y", "zh", "core"), ("x", "zl"), None)
    return jax.shard_map(
        on_device,
        mesh=parts,
        in_specs=(tiles,) + (P(),) * 10,
        out_specs=tiles,
        check_vma=False,
    )
```

```python
import functools
import math

import jax
import jax.numpy as jnp
from jax import lax
from jax.experimental import pallas as pl
from jax.experimental.pallas import tpu as pltpu
from jax.sharding import Mesh
from jax.sharding import PartitionSpec as P

F32 = jnp.float32
BF = jnp.bfloat16
CHUNKS = 2
TOGETHER = 2
DEPTH = 32


def dot(a, b):
    return jnp.dot(a, b, preferred_element_type=F32)


def dot_t(a, b):
    return lax.dot_general(a, b, (((1,), (1,)), ((), ())), preferred_element_type=F32)


def fold(function, so_far, value):
    return value if so_far is None else function(so_far, value)


def attend_kernel(
    at,
    x0,
    x1,
    x2,
    x3,
    b00,
    b01,
    b10,
    b11,
    b20,
    b21,
    b30,
    b31,
    w_key,
    w_value_t,
    w_query_t,
    w_gate_t,
    gate_shift,
    w_out,
    out_shift,
    out,
    key_ref,
    value_ref,
    score_ref,
    attended_ref,
):
    rows = (x0, x1, x2, x3)
    bias = ((b00, b01), (b10, b11), (b20, b21), (b30, b31))
    y, zl, core = at[0], at[2], at[3]
    slot = [lax.rem(zl + 4 - part, 4) for part in range(4)]
    heads = [lax.rem(y + 4 - step, 4) for step in range(4)]
    halves = [pl.multiple_of(lax.rem(core + half, 2) * 32, 32) for half in range(2)]
    kept = [{} for _ in range(TOGETHER)]

    def project_query(r):
        tokens = jnp.concatenate([x0[slot[part], r] for part in range(4)], axis=0)
        query = (dot_t(w_query_t[...], tokens) * (1.0 / math.sqrt(DEPTH))).astype(BF)
        gate = jax.nn.sigmoid(dot_t(w_gate_t[...], tokens) + gate_shift[...])
        of_head = lax.broadcasted_iota(jnp.int32, query.shape, 0) // DEPTH
        zero = jnp.zeros_like(query)
        return [jnp.where(of_head == head, query, zero) for head in heads], gate

    def project(r):
        tokens = jnp.concatenate(
            [
                rows[t][s, r, pl.ds(halves[half], 32), :]
                for half in range(2)
                for s in range(4)
                for t in range(4)
            ],
            axis=0,
        )
        key_ref[r] = dot(tokens, w_key[...]).astype(BF)
        value_ref[r] = dot_t(w_value_t[...], tokens).astype(BF)
        kept[r]["query"], kept[r]["gate"] = project_query(r)

    def score(r, a, c, query):
        half, s = divmod(c, 4)
        z_of = [zh * 4 + lax.rem(zl + 4 - s, 4) for zh in range(2)]
        added = jnp.concatenate([bias[a][half][z] for z in z_of], axis=1)
        return dot(key_ref[r, c * 128 : (c + 1) * 128, :], query[a]) + added

    def raise_plain(r, a):
        total = None
        for c in range(8):
            raised = jnp.exp(score(r, a, c, kept[r]["query"]))
            score_ref[r, a, c] = raised
            total = fold(jnp.add, total, jnp.sum(raised.reshape(16, 8, 256), axis=0))
        return jnp.sum(total, axis=0, keepdims=True)

    def raise_shifted(r, a, query):
        largest = None
        for c in range(8):
            scores = score(r, a, c, query)
            score_ref[r, a, c] = scores
            largest = fold(
                jnp.maximum, largest, jnp.max(scores.reshape(16, 8, 256), axis=0)
            )
        largest = jnp.max(largest, axis=0, keepdims=True)
        total = None
        for c in range(8):
            raised = jnp.exp(score_ref[r, a, c] - largest)
            score_ref[r, a, c] = raised
            total = fold(jnp.add, total, jnp.sum(raised.reshape(16, 8, 256), axis=0))
        return jnp.sum(total, axis=0, keepdims=True)

    def weigh(r, a, total):
        scale = 1.0 / total
        weights = jnp.concatenate(
            [(score_ref[r, a, c] * scale).astype(BF) for c in range(8)], axis=0
        )
        own = pl.ds(pl.multiple_of(heads[a] * DEPTH, DEPTH), DEPTH)
        attended_ref[r, own, :] = dot(value_ref[r, own, :], weights)

    def finish(r, gate):
        gated = (gate * attended_ref[r]).astype(BF)
        update = lax.dot_general(
            gated, w_out[...], (((0,), (0,)), ((), ())), preferred_element_type=F32
        )
        update = (update + out_shift[...]).astype(BF)
        for part in range(4):
            out[slot[part], r] = update[part * 64 : (part + 1) * 64]

    for r in range(TOGETHER):
        project(r)
    totals = {}
    for r in range(TOGETHER):
        for a in range(4):
            totals[r, a] = raise_plain(r, a)
    for r in range(TOGETHER):
        for a in range(4):
            weigh(r, a, totals[r, a])
    for r in range(TOGETHER):
        finish(r, kept[r]["gate"])

    safe = None
    for total in totals.values():
        inside = jnp.logical_and(total > 2.0**-60, total < 2.0**120)
        safe = fold(jnp.minimum, safe, jnp.where(inside, 1.0, 0.0))

    @pl.when(jnp.min(safe) < 0.5)
    def _():
        for r in range(TOGETHER):
            query, gate = project_query(r)
            for a in range(4):
                weigh(r, a, raise_shifted(r, a, query))
            finish(r, gate)


def attend(at, rows, first, biases, *weights):
    count = 16 // CHUNKS
    whole = lambda a: pl.BlockSpec(a.shape, lambda i, at: (0,) * a.ndim)
    block = (4, TOGETHER, 64, 128)
    specs = [
        pl.BlockSpec(block, lambda i, at, start=start // TOGETHER: (0, i + start, 0, 0))
        for start in first
    ]
    biases = [b for pair in biases for b in pair]
    return pl.pallas_call(
        attend_kernel,
        out_shape=jax.ShapeDtypeStruct((4, count, 64, 128), BF),
        grid_spec=pltpu.PrefetchScalarGridSpec(
            num_scalar_prefetch=1,
            grid=(count // TOGETHER,),
            in_specs=specs
            + [whole(a) for a in biases]
            + [whole(a) for a in weights],
            out_specs=pl.BlockSpec(block, lambda i, at: (0, i, 0, 0)),
            scratch_shapes=[
                pltpu.VMEM((TOGETHER, 1024, 128), BF),
                pltpu.VMEM((TOGETHER, 128, 1024), BF),
                pltpu.VMEM((TOGETHER, 4, 8, 128, 256), F32),
                pltpu.VMEM((TOGETHER, 128, 256), F32),
            ],
        ),
        compiler_params=pltpu.CompilerParams(
            vmem_limit_bytes=48 << 20, dimension_semantics=("arbitrary",)
        ),
        cost_estimate=pl.CostEstimate(
            flops=count * 300_000_000,
            bytes_accessed=count << 20,
            transcendentals=count << 20,
        ),
        name="attention",
    )(at, *rows, *biases, *weights)


def normalize(values, gain, shift):
    values = values.astype(F32)
    mean = jnp.mean(values, axis=-1, keepdims=True)
    centred = values - mean
    spread = jnp.mean(centred * centred, axis=-1, keepdims=True)
    return (centred * lax.rsqrt(spread + 1e-05) * gain + shift).astype(BF)


def assemble_kernel(at, *refs):
    *blocks, out = refs
    count = blocks[0].shape[0]
    for i, block in enumerate(blocks):
        chunk, step = divmod(i, 4)
        start = lax.rem(at[2] + step, 4) * 16 + chunk * count
        out[pl.ds(start, count)] = block[...]


def assemble(at, blocks):
    return pl.pallas_call(
        assemble_kernel,
        out_shape=jax.ShapeDtypeStruct((64, 64, 128), BF),
        in_specs=[pl.BlockSpec(memory_space=pltpu.SMEM)]
        + [pl.BlockSpec(memory_space=pltpu.VMEM)] * len(blocks),
        out_specs=pl.BlockSpec(memory_space=pltpu.VMEM),
        name="assemble_update",
    )(at, *blocks)


def tie_kernel(array, *rest):
    pass


def after(array, *earlier):
    return pl.pallas_call(
        tie_kernel,
        out_shape=jax.ShapeDtypeStruct(array.shape, array.dtype),
        in_specs=[pl.BlockSpec(memory_space=pl.ANY)] * (1 + len(earlier)),
        out_specs=pl.BlockSpec(memory_space=pl.ANY),
        input_output_aliases={0: 0},
        name="tie",
    )(array, *earlier)


AXES = ("y", "zh", "core", "x", "zl")


def move(array, to):
    pairs = []
    for source in range(256):
        row, col = divmod(source, 16)
        y, zh, core = row // 4, row // 2 % 2, row % 2
        x, zl = divmod(col, 4)
        y, z, core, x = to(y, zh * 4 + zl, core, x)
        y, z, x = y % 4, z % 8, x % 4
        target = ((y * 2 + z // 4) * 2 + core) * 16 + x * 4 + z % 4
        pairs.append((source, target))
    return lax.ppermute(array, AXES, pairs)


def swap_cores(array):
    return move(array, lambda y, z, core, x: (y, z, 1 - core, x))


def turn(z, step):
    return z // 4 * 4 + (z + step) % 4


def on_device(
    pair,
    norm_gain,
    norm_shift,
    w_query,
    w_key,
    w_value,
    w_gate,
    gate_shift,
    w_bias,
    w_out,
    out_shift,
):
    y, core, x, zl = (lax.axis_index(name) for name in ("y", "core", "x", "zl"))
    place = jnp.stack([y, x, zl, core]).astype(jnp.int32)
    normed = normalize(pair, norm_gain, norm_shift)
    count = 16 // CHUNKS

    with jax.named_scope("bias"):
        tile = jnp.einsum(
            "jkc,ch->hkj", normed.astype(F32), w_bias, precision=lax.Precision.HIGHEST
        )
        kept = lax.dynamic_slice_in_dim(tile, core * 32, 32, 1)
        sent = lax.dynamic_slice_in_dim(tile, (1 - core) * 32, 32, 1)
        got = swap_cores(sent)
        tile = jnp.where(
            core == 0, jnp.concatenate([kept, got], 2), jnp.concatenate([got, kept], 2)
        )
        rounds = []
        for step in range(4):
            part = lax.dynamic_index_in_dim(tile, (x + step) % 4, 0, keepdims=False)
            rounds.append(move(part, lambda y, z, core, x: (x + step, z, core, y)))
        rounds = jnp.stack(rounds + rounds[:3])
        block = lax.dynamic_slice_in_dim(rounds, (y - x) % 4, 4, 0).reshape(128, 128)
        turned = after(place, block)[2]
        pieces = []
        for step in range(4):
            part = lax.dynamic_slice_in_dim(normed, (turned + step) % 4 * 16, 16, 0)
            if step:
                part = move(part, lambda y, z, core, x: (y, turn(z, step), core, x))
            pieces.append(part)
        along_z = lax.all_to_all(
            jnp.broadcast_to(block[None], (8, 128, 128)),
            ("zh", "zl"),
            split_axis=0,
            concat_axis=0,
            tiled=True,
        )
    with jax.named_scope("rows"):
        here = jnp.stack(pieces)
        left = move(here, lambda y, z, core, x: (y, z, core, x + 1))
        right = move(here, lambda y, z, core, x: (y, z, core, x - 1))
        across = (
            move(left[:, :count], lambda y, z, core, x: (y, z, core, x + 1)),
            move(right[:, count:], lambda y, z, core, x: (y, z, core, x - 1)),
        )
    with jax.named_scope("bias"):
        along_z = after(along_z, *pieces[1:])
        biases = []
        for step in range(4):
            moved = along_z
            if step:
                moved = move(along_z, lambda y, z, core, x: (y + step, z, core, x))
            biases.append((moved, swap_cores(moved)))
    blocks = []
    for chunk in range(CHUNKS):
        with jax.named_scope("attention"):
            part = attend(
                place,
                (here, left, across[chunk], right),
                (chunk * count, chunk * count, 0, chunk * count),
                biases,
                w_key,
                w_value.T,
                w_query.T,
                w_gate.T,
                gate_shift[:, None],
                w_out,
                out_shift[None],
            )
            place = after(place, part)
        with jax.named_scope("update"):
            for step in range(4):
                back = part[step]
                if step:
                    back = move(back, lambda y, z, core, x: (y, turn(z, -step), core, x))
                blocks.append(back)
    return assemble(place, blocks)


def solution(mesh):
    parts = Mesh(mesh.devices.reshape(4, 2, 2, 4, 4), AXES)
    tiles = P(("y", "zh", "core"), ("x", "zl"), None)
    return jax.shard_map(
        on_device,
        mesh=parts,
        in_specs=(tiles,) + (P(),) * 10,
        out_specs=tiles,
        check_vma=False,
    )
```

```python
import functools
import math

import jax
import jax.numpy as jnp
from jax import lax
from jax.experimental import pallas as pl
from jax.experimental.pallas import tpu as pltpu
from jax.sharding import Mesh
from jax.sharding import PartitionSpec as P

F32 = jnp.float32
BF = jnp.bfloat16
CHUNKS = 2
TOGETHER = 4
DEPTH = 32


def dot(a, b):
    return jnp.dot(a, b, preferred_element_type=F32)


def dot_t(a, b):
    return lax.dot_general(a, b, (((1,), (1,)), ((), ())), preferred_element_type=F32)


def fold(function, so_far, value):
    return value if so_far is None else function(so_far, value)


def attend_kernel(
    at,
    x0,
    x1,
    x2,
    x3,
    b00,
    b01,
    b10,
    b11,
    b20,
    b21,
    b30,
    b31,
    w_key,
    w_value_t,
    w_query_t,
    w_gate_t,
    gate_shift,
    w_out,
    out_shift,
    out,
    key_ref,
    value_ref,
    score_ref,
    attended_ref,
):
    rows = (x0, x1, x2, x3)
    bias = ((b00, b01), (b10, b11), (b20, b21), (b30, b31))
    y, zl, core = at[0], at[2], at[3]
    slot = [lax.rem(zl + 4 - part, 4) for part in range(4)]
    heads = [lax.rem(y + 4 - step, 4) for step in range(4)]
    halves = [pl.multiple_of(lax.rem(core + half, 2) * 32, 32) for half in range(2)]
    kept = [{} for _ in range(TOGETHER)]

    def project_query(r):
        tokens = jnp.concatenate([x0[slot[part], r] for part in range(4)], axis=0)
        query = (dot_t(w_query_t[...], tokens) * (1.0 / math.sqrt(DEPTH))).astype(BF)
        gate = jax.nn.sigmoid(dot_t(w_gate_t[...], tokens) + gate_shift[...])
        of_head = lax.broadcasted_iota(jnp.int32, query.shape, 0) // DEPTH
        zero = jnp.zeros_like(query)
        return [jnp.where(of_head == head, query, zero) for head in heads], gate

    def project(r):
        tokens = jnp.concatenate(
            [
                rows[t][s, r, pl.ds(halves[half], 32), :]
                for half in range(2)
                for s in range(4)
                for t in range(4)
            ],
            axis=0,
        )
        key_ref[r] = dot(tokens, w_key[...]).astype(BF)
        value_ref[r] = dot_t(w_value_t[...], tokens).astype(BF)
        kept[r]["query"], kept[r]["gate"] = project_query(r)

    def score(r, a, c, query):
        half, s = divmod(c, 4)
        z_of = [zh * 4 + lax.rem(zl + 4 - s, 4) for zh in range(2)]
        added = jnp.concatenate([bias[a][half][z] for z in z_of], axis=1)
        return dot(key_ref[r, c * 128 : (c + 1) * 128, :], query[a]) + added

    def raise_plain(r, a):
        total = None
        for c in range(8):
            raised = jnp.exp(score(r, a, c, kept[r]["query"]))
            score_ref[r, a, c] = raised
            total = fold(jnp.add, total, jnp.sum(raised.reshape(16, 8, 256), axis=0))
        return jnp.sum(total, axis=0, keepdims=True)

    def raise_shifted(r, a, query):
        largest = None
        for c in range(8):
            scores = score(r, a, c, query)
            score_ref[r, a, c] = scores
            largest = fold(
                jnp.maximum, largest, jnp.max(scores.reshape(16, 8, 256), axis=0)
            )
        largest = jnp.max(largest, axis=0, keepdims=True)
        total = None
        for c in range(8):
            raised = jnp.exp(score_ref[r, a, c] - largest)
            score_ref[r, a, c] = raised
            total = fold(jnp.add, total, jnp.sum(raised.reshape(16, 8, 256), axis=0))
        return jnp.sum(total, axis=0, keepdims=True)

    def weigh(r, a, total):
        scale = 1.0 / total
        weights = jnp.concatenate(
            [(score_ref[r, a, c] * scale).astype(BF) for c in range(8)], axis=0
        )
        own = pl.ds(pl.multiple_of(heads[a] * DEPTH, DEPTH), DEPTH)
        attended_ref[r, own, :] = dot(value_ref[r, own, :], weights)

    def finish(r, gate):
        gated = (gate * attended_ref[r]).astype(BF)
        update = lax.dot_general(
            gated, w_out[...], (((0,), (0,)), ((), ())), preferred_element_type=F32
        )
        update = (update + out_shift[...]).astype(BF)
        for part in range(4):
            out[slot[part], r] = update[part * 64 : (part + 1) * 64]

    for r in range(TOGETHER):
        project(r)
    totals = {}
    for r in range(TOGETHER):
        for a in range(4):
            totals[r, a] = raise_plain(r, a)
    for r in range(TOGETHER):
        for a in range(4):
            weigh(r, a, totals[r, a])
    for r in range(TOGETHER):
        finish(r, kept[r]["gate"])

    safe = None
    for total in totals.values():
        inside = jnp.logical_and(total > 2.0**-60, total < 2.0**120)
        safe = fold(jnp.minimum, safe, jnp.where(inside, 1.0, 0.0))

    @pl.when(jnp.min(safe) < 0.5)
    def _():
        for r in range(TOGETHER):
            query, gate = project_query(r)
            for a in range(4):
                weigh(r, a, raise_shifted(r, a, query))
            finish(r, gate)


def attend(at, rows, first, biases, *weights):
    count = 16 // CHUNKS
    whole = lambda a: pl.BlockSpec(a.shape, lambda i, at: (0,) * a.ndim)
    block = (4, TOGETHER, 64, 128)
    specs = [
        pl.BlockSpec(block, lambda i, at, start=start // TOGETHER: (0, i + start, 0, 0))
        for start in first
    ]
    biases = [b for pair in biases for b in pair]
    return pl.pallas_call(
        attend_kernel,
        out_shape=jax.ShapeDtypeStruct((4, count, 64, 128), BF),
        grid_spec=pltpu.PrefetchScalarGridSpec(
            num_scalar_prefetch=1,
            grid=(count // TOGETHER,),
            in_specs=specs
            + [whole(a) for a in biases]
            + [whole(a) for a in weights],
            out_specs=pl.BlockSpec(block, lambda i, at: (0, i, 0, 0)),
            scratch_shapes=[
                pltpu.VMEM((TOGETHER, 1024, 128), BF),
                pltpu.VMEM((TOGETHER, 128, 1024), BF),
                pltpu.VMEM((TOGETHER, 4, 8, 128, 256), F32),
                pltpu.VMEM((TOGETHER, 128, 256), F32),
            ],
        ),
        compiler_params=pltpu.CompilerParams(
            vmem_limit_bytes=48 << 20, dimension_semantics=("arbitrary",)
        ),
        cost_estimate=pl.CostEstimate(
            flops=count * 300_000_000,
            bytes_accessed=count << 20,
            transcendentals=count << 20,
        ),
        name="attention",
    )(at, *rows, *biases, *weights)


def normalize(values, gain, shift):
    values = values.astype(F32)
    mean = jnp.mean(values, axis=-1, keepdims=True)
    centred = values - mean
    spread = jnp.mean(centred * centred, axis=-1, keepdims=True)
    return (centred * lax.rsqrt(spread + 1e-05) * gain + shift).astype(BF)


def assemble_kernel(at, *refs):
    *blocks, out = refs
    count = blocks[0].shape[0]
    for i, block in enumerate(blocks):
        chunk, step = divmod(i, 4)
        start = lax.rem(at[2] + step, 4) * 16 + chunk * count
        out[pl.ds(start, count)] = block[...]


def assemble(at, blocks):
    return pl.pallas_call(
        assemble_kernel,
        out_shape=jax.ShapeDtypeStruct((64, 64, 128), BF),
        in_specs=[pl.BlockSpec(memory_space=pltpu.SMEM)]
        + [pl.BlockSpec(memory_space=pltpu.VMEM)] * len(blocks),
        out_specs=pl.BlockSpec(memory_space=pltpu.VMEM),
        name="assemble_update",
    )(at, *blocks)


def tie_kernel(array, *rest):
    pass


def after(array, *earlier):
    return pl.pallas_call(
        tie_kernel,
        out_shape=jax.ShapeDtypeStruct(array.shape, array.dtype),
        in_specs=[pl.BlockSpec(memory_space=pl.ANY)] * (1 + len(earlier)),
        out_specs=pl.BlockSpec(memory_space=pl.ANY),
        input_output_aliases={0: 0},
        name="tie",
    )(array, *earlier)


AXES = ("y", "zh", "core", "x", "zl")


def move(array, to):
    pairs = []
    for source in range(256):
        row, col = divmod(source, 16)
        y, zh, core = row // 4, row // 2 % 2, row % 2
        x, zl = divmod(col, 4)
        y, z, core, x = to(y, zh * 4 + zl, core, x)
        y, z, x = y % 4, z % 8, x % 4
        target = ((y * 2 + z // 4) * 2 + core) * 16 + x * 4 + z % 4
        pairs.append((source, target))
    return lax.ppermute(array, AXES, pairs)


def swap_cores(array):
    return move(array, lambda y, z, core, x: (y, z, 1 - core, x))


def turn(z, step):
    return z // 4 * 4 + (z + step) % 4


def on_device(
    pair,
    norm_gain,
    norm_shift,
    w_query,
    w_key,
    w_value,
    w_gate,
    gate_shift,
    w_bias,
    w_out,
    out_shift,
):
    y, core, x, zl = (lax.axis_index(name) for name in ("y", "core", "x", "zl"))
    place = jnp.stack([y, x, zl, core]).astype(jnp.int32)
    normed = normalize(pair, norm_gain, norm_shift)
    count = 16 // CHUNKS

    with jax.named_scope("rows"):
        pieces = []
        for step in range(4):
            part = lax.dynamic_slice_in_dim(normed, (zl + step) % 4 * 16, 16, 0)
            if step:
                part = move(part, lambda y, z, core, x: (y, turn(z, step), core, x))
            pieces.append(part)
        here = jnp.stack(pieces)
        left = move(here, lambda y, z, core, x: (y, z, core, x + 1))
        right = move(here, lambda y, z, core, x: (y, z, core, x - 1))
        across = (
            move(left[:, :count], lambda y, z, core, x: (y, z, core, x + 1)),
            move(right[:, count:], lambda y, z, core, x: (y, z, core, x - 1)),
        )
    with jax.named_scope("bias"):
        tile = jnp.einsum(
            "jkc,ch->hkj", normed.astype(F32), w_bias, precision=lax.Precision.HIGHEST
        )
        kept = lax.dynamic_slice_in_dim(tile, core * 32, 32, 1)
        sent = lax.dynamic_slice_in_dim(tile, (1 - core) * 32, 32, 1)
        got = swap_cores(sent)
        tile = jnp.where(
            core == 0, jnp.concatenate([kept, got], 2), jnp.concatenate([got, kept], 2)
        )
        rounds = []
        for step in range(4):
            part = lax.dynamic_index_in_dim(tile, (x + step) % 4, 0, keepdims=False)
            rounds.append(move(part, lambda y, z, core, x: (x + step, z, core, y)))
        rounds = jnp.stack(rounds + rounds[:3])
        block = lax.dynamic_slice_in_dim(rounds, (y - x) % 4, 4, 0).reshape(128, 128)
        block = after(block, here)
        along_z = lax.all_to_all(
            jnp.broadcast_to(block[None], (8, 128, 128)),
            ("zh", "zl"),
            split_axis=0,
            concat_axis=0,
            tiled=True,
        )
    with jax.named_scope("bias"):
        along_z = after(along_z, left, right)
        biases = []
        for step in range(4):
            moved = along_z
            if step:
                moved = move(along_z, lambda y, z, core, x: (y + step, z, core, x))
            biases.append((moved, swap_cores(moved)))
    blocks = []
    for chunk in range(CHUNKS):
        with jax.named_scope("attention"):
            part = attend(
                place,
                (here, left, across[chunk], right),
                (chunk * count, chunk * count, 0, chunk * count),
                biases,
                w_key,
                w_value.T,
                w_query.T,
                w_gate.T,
                gate_shift[:, None],
                w_out,
                out_shift[None],
            )
            place = after(place, part)
        with jax.named_scope("update"):
            for step in range(4):
                back = part[step]
                if step:
                    back = move(back, lambda y, z, core, x: (y, turn(z, -step), core, x))
                blocks.append(back)
    return assemble(place, blocks)


def solution(mesh):
    parts = Mesh(mesh.devices.reshape(4, 2, 2, 4, 4), AXES)
    tiles = P(("y", "zh", "core"), ("x", "zl"), None)
    return jax.shard_map(
        on_device,
        mesh=parts,
        in_specs=(tiles,) + (P(),) * 10,
        out_specs=tiles,
        check_vma=False,
    )
```

```python
import functools
import math

import jax
import jax.numpy as jnp
from jax import lax
from jax.experimental import pallas as pl
from jax.experimental.pallas import tpu as pltpu
from jax.sharding import Mesh
from jax.sharding import PartitionSpec as P

F32 = jnp.float32
BF = jnp.bfloat16
CHUNKS = 2
TOGETHER = 2
DEPTH = 32


def dot(a, b):
    return jnp.dot(a, b, preferred_element_type=F32)


def dot_t(a, b):
    return lax.dot_general(a, b, (((1,), (1,)), ((), ())), preferred_element_type=F32)


def fold(function, so_far, value):
    return value if so_far is None else function(so_far, value)


def attend_kernel(
    at,
    x0,
    x1,
    x2,
    x3,
    b00,
    b01,
    b10,
    b11,
    b20,
    b21,
    b30,
    b31,
    w_key,
    w_value_t,
    w_query_t,
    w_gate_t,
    gate_shift,
    w_out,
    out_shift,
    out,
    key_ref,
    value_ref,
    score_ref,
    attended_ref,
):
    rows = (x0, x1, x2, x3)
    bias = ((b00, b01), (b10, b11), (b20, b21), (b30, b31))
    y, zl, core = at[0], at[2], at[3]
    slot = [lax.rem(zl + 4 - part, 4) for part in range(4)]
    heads = [lax.rem(y + 4 - step, 4) for step in range(4)]
    halves = [pl.multiple_of(lax.rem(core + half, 2) * 32, 32) for half in range(2)]
    kept = [{} for _ in range(TOGETHER)]

    def project_query(r):
        tokens = jnp.concatenate([x0[slot[part], r] for part in range(4)], axis=0)
        query = (dot_t(w_query_t[...], tokens) * (1.0 / math.sqrt(DEPTH))).astype(BF)
        gate = jax.nn.sigmoid(dot_t(w_gate_t[...], tokens) + gate_shift[...])
        of_head = lax.broadcasted_iota(jnp.int32, query.shape, 0) // DEPTH
        zero = jnp.zeros_like(query)
        return [jnp.where(of_head == head, query, zero) for head in heads], gate

    def project(r):
        tokens = jnp.concatenate(
            [
                rows[t][s, r, pl.ds(halves[half], 32), :]
                for half in range(2)
                for s in range(4)
                for t in range(4)
            ],
            axis=0,
        )
        key_ref[r] = dot(tokens, w_key[...]).astype(BF)
        value_ref[r] = dot_t(w_value_t[...], tokens).astype(BF)
        kept[r]["query"], kept[r]["gate"] = project_query(r)

    def score(r, a, c, query):
        half, s = divmod(c, 4)
        z_of = [zh * 4 + lax.rem(zl + 4 - s, 4) for zh in range(2)]
        added = jnp.concatenate([bias[a][half][z] for z in z_of], axis=1)
        return dot(key_ref[r, c * 128 : (c + 1) * 128, :], query[a]) + added

    def raise_plain(r, a):
        total = None
        for c in range(8):
            raised = jnp.exp(score(r, a, c, kept[r]["query"]))
            score_ref[r, a, c] = raised
            total = fold(jnp.add, total, jnp.sum(raised.reshape(16, 8, 256), axis=0))
        return jnp.sum(total, axis=0, keepdims=True)

    def raise_shifted(r, a, query):
        largest = None
        for c in range(8):
            scores = score(r, a, c, query)
            score_ref[r, a, c] = scores
            largest = fold(
                jnp.maximum, largest, jnp.max(scores.reshape(16, 8, 256), axis=0)
            )
        largest = jnp.max(largest, axis=0, keepdims=True)
        total = None
        for c in range(8):
            raised = jnp.exp(score_ref[r, a, c] - largest)
            score_ref[r, a, c] = raised
            total = fold(jnp.add, total, jnp.sum(raised.reshape(16, 8, 256), axis=0))
        return jnp.sum(total, axis=0, keepdims=True)

    def weigh(r, a, total):
        scale = 1.0 / total
        weights = jnp.concatenate(
            [(score_ref[r, a, c] * scale).astype(BF) for c in range(8)], axis=0
        )
        own = pl.ds(pl.multiple_of(heads[a] * DEPTH, DEPTH), DEPTH)
        attended_ref[r, own, :] = dot(value_ref[r, own, :], weights)

    def finish(r, gate):
        gated = (gate * attended_ref[r]).astype(BF)
        update = lax.dot_general(
            gated, w_out[...], (((0,), (0,)), ((), ())), preferred_element_type=F32
        )
        update = (update + out_shift[...]).astype(BF)
        for part in range(4):
            out[slot[part], r] = update[part * 64 : (part + 1) * 64]

    for r in range(TOGETHER):
        project(r)
    totals = {}
    for r in range(TOGETHER):
        for a in range(4):
            totals[r, a] = raise_plain(r, a)
    for r in range(TOGETHER):
        for a in range(4):
            weigh(r, a, totals[r, a])
    for r in range(TOGETHER):
        finish(r, kept[r]["gate"])

    safe = None
    for total in totals.values():
        inside = jnp.logical_and(total > 2.0**-60, total < 2.0**120)
        safe = fold(jnp.minimum, safe, jnp.where(inside, 1.0, 0.0))

    @pl.when(jnp.min(safe) < 0.5)
    def _():
        for r in range(TOGETHER):
            query, gate = project_query(r)
            for a in range(4):
                weigh(r, a, raise_shifted(r, a, query))
            finish(r, gate)


def attend(at, rows, first, biases, *weights):
    count = 16 // CHUNKS
    whole = lambda a: pl.BlockSpec(a.shape, lambda i, at: (0,) * a.ndim)
    block = (4, TOGETHER, 64, 128)
    start = first // TOGETHER
    specs = [pl.BlockSpec(block, lambda i, at: (0, i + start, 0, 0))] * 4
    biases = [b for pair in biases for b in pair]
    return pl.pallas_call(
        attend_kernel,
        out_shape=jax.ShapeDtypeStruct((4, count, 64, 128), BF),
        grid_spec=pltpu.PrefetchScalarGridSpec(
            num_scalar_prefetch=1,
            grid=(count // TOGETHER,),
            in_specs=specs
            + [whole(a) for a in biases]
            + [whole(a) for a in weights],
            out_specs=pl.BlockSpec(block, lambda i, at: (0, i, 0, 0)),
            scratch_shapes=[
                pltpu.VMEM((TOGETHER, 1024, 128), BF),
                pltpu.VMEM((TOGETHER, 128, 1024), BF),
                pltpu.VMEM((TOGETHER, 4, 8, 128, 256), F32),
                pltpu.VMEM((TOGETHER, 128, 256), F32),
            ],
        ),
        compiler_params=pltpu.CompilerParams(
            vmem_limit_bytes=48 << 20, dimension_semantics=("arbitrary",)
        ),
        cost_estimate=pl.CostEstimate(
            flops=count * 300_000_000,
            bytes_accessed=count << 20,
            transcendentals=count << 20,
        ),
        name="attention",
    )(at, *rows, *biases, *weights)


def normalize(values, gain, shift):
    values = values.astype(F32)
    mean = jnp.mean(values, axis=-1, keepdims=True)
    centred = values - mean
    spread = jnp.mean(centred * centred, axis=-1, keepdims=True)
    return (centred * lax.rsqrt(spread + 1e-05) * gain + shift).astype(BF)


def assemble_kernel(at, *refs):
    *blocks, out = refs
    count = blocks[0].shape[0]
    for i, block in enumerate(blocks):
        chunk, step = divmod(i, 4)
        start = lax.rem(at[2] + step, 4) * 16 + chunk * count
        out[pl.ds(start, count)] = block[...]


def assemble(at, blocks):
    return pl.pallas_call(
        assemble_kernel,
        out_shape=jax.ShapeDtypeStruct((64, 64, 128), BF),
        in_specs=[pl.BlockSpec(memory_space=pltpu.SMEM)]
        + [pl.BlockSpec(memory_space=pltpu.VMEM)] * len(blocks),
        out_specs=pl.BlockSpec(memory_space=pltpu.VMEM),
        name="assemble_update",
    )(at, *blocks)


def tie_kernel(array, *rest):
    pass


def after(array, *earlier, where=pltpu.VMEM):
    return pl.pallas_call(
        tie_kernel,
        out_shape=jax.ShapeDtypeStruct(array.shape, array.dtype),
        in_specs=[pl.BlockSpec(memory_space=pl.ANY)]
        + [pl.BlockSpec(memory_space=where)] * len(earlier),
        out_specs=pl.BlockSpec(memory_space=pl.ANY),
        input_output_aliases={0: 0},
        name="tie",
    )(array, *earlier)


AXES = ("y", "zh", "core", "x", "zl")


def move(array, to):
    pairs = []
    for source in range(256):
        row, col = divmod(source, 16)
        y, zh, core = row // 4, row // 2 % 2, row % 2
        x, zl = divmod(col, 4)
        y, z, core, x = to(y, zh * 4 + zl, core, x)
        y, z, x = y % 4, z % 8, x % 4
        target = ((y * 2 + z // 4) * 2 + core) * 16 + x * 4 + z % 4
        pairs.append((source, target))
    return lax.ppermute(array, AXES, pairs)


def swap_cores(array):
    return move(array, lambda y, z, core, x: (y, z, 1 - core, x))


def turn(z, step):
    return z // 4 * 4 + (z + step) % 4


def on_device(
    pair,
    norm_gain,
    norm_shift,
    w_query,
    w_key,
    w_value,
    w_gate,
    gate_shift,
    w_bias,
    w_out,
    out_shift,
):
    y, core, x, zl = (lax.axis_index(name) for name in ("y", "core", "x", "zl"))
    place = jnp.stack([y, x, zl, core]).astype(jnp.int32)
    normed = normalize(pair, norm_gain, norm_shift)
    count = 16 // CHUNKS

    with jax.named_scope("rows"):
        pieces = []
        for step in range(4):
            part = lax.dynamic_slice_in_dim(normed, (zl + step) % 4 * 16, 16, 0)
            if step:
                part = move(part, lambda y, z, core, x: (y, turn(z, step), core, x))
            pieces.append(part)
        here = jnp.stack(pieces)
        left = move(here, lambda y, z, core, x: (y, z, core, x + 1))
        right = move(here, lambda y, z, core, x: (y, z, core, x - 1))
        across = move(here, lambda y, z, core, x: (y, z, core, x + 2))
    with jax.named_scope("bias"):
        tile = jnp.einsum(
            "jkc,ch->hkj", normed.astype(F32), w_bias, precision=lax.Precision.HIGHEST
        )
        kept = lax.dynamic_slice_in_dim(tile, core * 32, 32, 1)
        sent = lax.dynamic_slice_in_dim(tile, (1 - core) * 32, 32, 1)
        got = swap_cores(sent)
        tile = jnp.where(
            core == 0, jnp.concatenate([kept, got], 2), jnp.concatenate([got, kept], 2)
        )
        rounds = []
        for step in range(4):
            part = lax.dynamic_index_in_dim(tile, (x + step) % 4, 0, keepdims=False)
            rounds.append(move(part, lambda y, z, core, x: (x + step, z, core, y)))
        rounds = jnp.stack(rounds + rounds[:3])
        block = lax.dynamic_slice_in_dim(rounds, (y - x) % 4, 4, 0).reshape(128, 128)
        block = after(block, here)
        along_z = lax.all_to_all(
            jnp.broadcast_to(block[None], (8, 128, 128)),
            ("zh", "zl"),
            split_axis=0,
            concat_axis=0,
            tiled=True,
        )
    with jax.named_scope("bias"):
        along_z = after(along_z, left, right)
        biases = []
        for step in range(4):
            moved = along_z
            if step:
                moved = move(along_z, lambda y, z, core, x: (y + step, z, core, x))
            biases.append((moved, swap_cores(moved)))
    blocks = []
    for chunk in range(CHUNKS):
        with jax.named_scope("attention"):
            part = attend(
                place,
                (here, left, across, right),
                chunk * count,
                biases,
                w_key,
                w_value.T,
                w_query.T,
                w_gate.T,
                gate_shift[:, None],
                w_out,
                out_shift[None],
            )
            place = after(place, part, where=pl.ANY)
        with jax.named_scope("update"):
            for step in range(4):
                back = part[step]
                if step:
                    back = move(back, lambda y, z, core, x: (y, turn(z, -step), core, x))
                blocks.append(back)
    return assemble(place, blocks)


def solution(mesh):
    parts = Mesh(mesh.devices.reshape(4, 2, 2, 4, 4), AXES)
    tiles = P(("y", "zh", "core"), ("x", "zl"), None)
    return jax.shard_map(
        on_device,
        mesh=parts,
        in_specs=(tiles,) + (P(),) * 10,
        out_specs=tiles,
        check_vma=False,
    )
```
